32 devices in a mesh: section: 4 (over z), dp: 8 (over y, x, core).
Axes of the slice: x: 2, y: 2, z: 4, core: 2. Of those that a mesh axis runs over, the one named last changes fastest.
Arguments:
- pending_predecessor_pair: float32 [4, 2, 8, 16, 16, 512], P('section', None, 'dp'), may hold values from -6 to 6
- incoming_stem_images: float32 [3, 8, 16, 16, 512], P(None, 'dp'), may hold values from -6 to 6
- spatial_filter_entries: float32 [4, 4, 9, 512], P('section', None, None, 'dp'), may hold values from -2 to 2
- mixing_matrix_entries: float32 [4, 4, 512, 512], P('section', None, 'dp'), may hold values from -0.25 to 0.25
Outputs:
- emitted: float32 [4, 4, 8, 16, 16, 512], P('section', None, 'dp')
The draws below stay inside these ranges and needn't reach their ends.
All inputs are finite; a program needn't handle non-finite values.
Results may differ from the reference program's by a relative error of at most 0.00015.
Values sent between devices are 32-bit elements; how exact they have to be, the bound alone decides.
No kernel may reach another device: no remote copies, remote signals or barrier semaphores. Data moves between devices by JAX's collectives and lax.ppermute only.
A program may use at most 64 MiB of HBM per device.

```python
import jax
import jax.numpy as jnp
from jax import lax

FILTER_NUMBER = 512
GRID_EXTENT = 16
TICKS = 4
CASCADE_LENGTH = 4
IMAGE_GROUP = 8


def levels(rng, extent, split, low, top_value):
    def one(dim, shards_of):
        steps = jax.random.uniform(jax.random.fold_in(jax.random.fold_in(rng, 6), dim), (shards_of,), jnp.float32, low / len(split), top_value / len(split))
        return jnp.repeat(jnp.exp(steps), extent[dim] // shards_of).reshape((-1,) + (1,) * (len(extent) - dim - 1))

    loudness = one(*split[0])
    for cut in split[1:]:
        loudness = loudness * one(*cut)
    return loudness


def normal_values(stream_key, dims, width, limit, cuts=(), dtype=jnp.bfloat16):
    loudness = levels(stream_key, dims, cuts, -0.22, 0.18) if cuts else 1.0
    array = jax.random.normal(stream_key, dims, jnp.float32) * width * loudness
    return jnp.minimum(jnp.maximum(array, -limit), limit).astype(dtype)


def setup_inputs(seed: int = 0) -> dict:
    seeds = jax.random.split(jax.random.key(seed), 5)
    return {
        "pending_predecessor_pair": normal_values(seeds[0], (CASCADE_LENGTH, 2, IMAGE_GROUP, GRID_EXTENT, GRID_EXTENT, FILTER_NUMBER), 1.0, 6.0, ((0, 4), (2, 8)), jnp.float32),
        "incoming_stem_images": normal_values(seeds[1], (TICKS - 1, IMAGE_GROUP, GRID_EXTENT, GRID_EXTENT, FILTER_NUMBER), 1.0, 6.0, ((1, 8),), jnp.float32),
        "spatial_filter_entries": normal_values(seeds[2], (CASCADE_LENGTH, 4, 9, FILTER_NUMBER), 0.333, 2.0, ((0, 4), (3, 8)), jnp.float32),
        "mixing_matrix_entries": normal_values(seeds[3], (CASCADE_LENGTH, 4, FILTER_NUMBER, FILTER_NUMBER), FILTER_NUMBER ** -0.5, 0.25, ((0, 4), (2, 8)), jnp.float32),
    }


def depthwise(source, tap_table):
    side = source.shape[1]
    padded = jnp.pad(source, ((0, 0), (1, 1), (1, 1), (0, 0)))
    running = jnp.zeros(source.shape, jnp.float32)
    for row_off in range(3):
        for col_off in range(3):
            running = running + padded[:, row_off:row_off + side, col_off:col_off + side, :] * tap_table[3 * row_off + col_off]
    return running


def separable(source, tap_table, kernel):
    mixed_in = depthwise(jnp.maximum(source, 0.0), tap_table)
    flattened = mixed_in.reshape(-1, mixed_in.shape[-1])
    result = jnp.dot(flattened, kernel, precision=lax.Precision.HIGHEST, preferred_element_type=jnp.float32)
    return result.reshape(source.shape)


def amoeba_cell(operands):
    prior_carry_output, current_carry_output, tap_table, kernels = operands
    sum_one = separable(current_carry_output, tap_table[0], kernels[0]) + separable(prior_carry_output, tap_table[1], kernels[1])
    sum_two = separable(sum_one, tap_table[2], kernels[2]) + current_carry_output
    return separable(sum_two, tap_table[3], kernels[3]) + sum_one


def reference(pending_predecessor_pair, incoming_stem_images, spatial_filter_entries, mixing_matrix_entries):
    prior_carry_output = pending_predecessor_pair[:, 0]
    current_carry_output = pending_predecessor_pair[:, 1]
    history = []
    for tick in range(TICKS):
        output = lax.map(amoeba_cell, (prior_carry_output, current_carry_output, spatial_filter_entries, mixing_matrix_entries))
        history.append(output)
        if tick < TICKS - 1:
            entering = incoming_stem_images[tick][None]
            prior_carry_output = jnp.concatenate([entering, current_carry_output[:-1]], axis=0)
            current_carry_output = jnp.concatenate([entering, output[:-1]], axis=0)
    return jnp.stack(history, axis=1)
```

```python
import functools

import jax
import jax.numpy as jnp
from jax import lax
from jax.experimental import pallas as pl
from jax.experimental.pallas import tpu as pltpu
from jax.sharding import PartitionSpec as P

F32 = jnp.float32
BF16 = jnp.bfloat16
VMEM_LIMIT = 32 * 1024 * 1024
WHOLE = pl.BlockSpec(memory_space=pltpu.VMEM)
SCALAR = pl.BlockSpec(memory_space=pltpu.SMEM)
ANY = pl.BlockSpec(memory_space=pl.ANY)


def swap(x, axis, bit):
    size = lax.axis_size(axis)
    return lax.ppermute(x, axis, [(i, i ^ bit) for i in range(size)])


def from_behind(x, axis, first=0):
    size = lax.axis_size(axis)
    return lax.ppermute(x, axis, [(i, i + 1) for i in range(first, size - 1)])


def split(x):
    high = x.astype(BF16)
    return high, (x - high.astype(F32)).astype(BF16)


def shifted(u, by):
    side = u.shape[1]
    column = lax.broadcasted_iota(jnp.int32, u.shape, 1)
    outside = 0 if by == 1 else side - 1
    return jnp.where(column == outside, 0.0, pltpu.roll(u, by % side, 1))


def depthwise(source, taps, branch, low, width):
    x = jnp.maximum(source[:, :, low : low + width], 0.0)
    nothing = jnp.zeros((1,) + x.shape[1:], F32)
    above = jnp.concatenate([nothing, x[:-1]], 0)
    below = jnp.concatenate([x[1:], nothing], 0)
    tap = [taps[branch, k : k + 1, low : low + width].reshape(1, 1, width) for k in range(9)]
    by_column = [above * tap[j] + x * tap[3 + j] + below * tap[6 + j] for j in range(3)]
    return shifted(by_column[0], 1) + by_column[1] + shifted(by_column[2], -1)


def separable(source, taps, highs, lows, branch):
    rows, columns, channels = source.shape
    width = min(128, channels)
    depth = min(256, channels)
    total = None
    for k in range(0, channels, depth):
        parts = []
        for low in range(k, k + depth, width):
            mixed_in = depthwise(source, taps, branch, low, width)
            parts.append(split(mixed_in.reshape(rows * columns, width)))
        high = jnp.concatenate([p[0] for p in parts], 1)
        low = jnp.concatenate([p[1] for p in parts], 1)
        matrix_high = highs[branch, k : k + depth, :]
        matrix_low = lows[branch, k : k + depth, :]
        product = jnp.dot(high, matrix_high, preferred_element_type=F32)
        product = product + jnp.dot(low, matrix_high, preferred_element_type=F32)
        product = product + jnp.dot(high, matrix_low, preferred_element_type=F32)
        total = product if total is None else total + product
    return total.reshape(source.shape)


def fetch(tick, at, section, stems, got, held, sem):
    for s in range(at):

        @pl.when(section == s)
        def _(s=s):
            copy = pltpu.make_async_copy(stems.at[tick - 1 - s], held, sem)
            copy.start()
            copy.wait()

    @pl.when(section >= at)
    def _():
        copy = pltpu.make_async_copy(got, held, sem)
        copy.start()
        copy.wait()


def early_kernel(tick, section, stems, got, taps, highs, lows, out, held, sem):
    fetch(tick, min(tick, 2), section[0], stems, got, held, sem)
    out[...] = separable(held, taps, highs, lows, 1)


def late_kernel(tick, n_past, section, stems, got, early, taps, highs, lows, *rest):
    past, (out, newest, first, second, sem, past_sem) = rest[:n_past], rest[n_past:]
    copies = [pltpu.make_async_copy(p, out.at[i], past_sem.at[i]) for i, p in enumerate(past)]
    for copy in copies:
        copy.start()
    fetch(tick, min(tick, 1), section[0], stems, got, newest, sem)
    first[...] = separable(newest, taps, highs, lows, 0) + early[...]
    second[...] = separable(first, taps, highs, lows, 2) + newest[...]
    output = separable(second, taps, highs, lows, 3) + first[...]
    if n_past:
        second[...] = output
        last = pltpu.make_async_copy(second, out.at[n_past], sem)
        last.start()
        last.wait()
    else:
        out[...] = output
    for copy in copies:
        copy.wait()


def cost(maps, convolutions):
    rows, columns, channels = maps
    size = rows * columns * channels
    return pl.CostEstimate(
        flops=6 * convolutions * size * channels,
        bytes_accessed=4 * (3 * size + convolutions * channels * channels),
        transcendentals=0,
    )


def early_part(tick, section, stems, got, taps, highs, lows):
    shape = got.shape
    return pl.pallas_call(
        functools.partial(early_kernel, tick),
        out_shape=jax.ShapeDtypeStruct(shape, F32),
        in_specs=[SCALAR, ANY, ANY, WHOLE, WHOLE, WHOLE],
        out_specs=WHOLE,
        scratch_shapes=[pltpu.VMEM(shape, F32), pltpu.SemaphoreType.DMA],
        compiler_params=pltpu.CompilerParams(vmem_limit_bytes=VMEM_LIMIT),
        cost_estimate=cost(shape, 1),
    )(section, stems, got, taps, highs, lows)


def late_part(tick, section, stems, got, early, taps, highs, lows, past=()):
    shape = got.shape
    n = len(past)
    return pl.pallas_call(
        functools.partial(late_kernel, tick, n),
        out_shape=jax.ShapeDtypeStruct((n + 1,) + shape if n else shape, F32),
        in_specs=[SCALAR, ANY, ANY, WHOLE, WHOLE, WHOLE, WHOLE] + [ANY] * n,
        out_specs=ANY if n else WHOLE,
        scratch_shapes=[pltpu.VMEM(shape, F32)] * 3
        + [pltpu.SemaphoreType.DMA, pltpu.SemaphoreType.DMA((max(n, 1),))],
        compiler_params=pltpu.CompilerParams(vmem_limit_bytes=VMEM_LIMIT),
        cost_estimate=cost(shape, 3),
    )(section, stems, got, early, taps, highs, lows, *past)


def prepare_kernel(bits, position, *refs):
    pieces, (highs, lows) = refs[:-2], refs[-2:]
    count = pieces[0].shape[1]
    for bit, piece in zip(bits, pieces):
        row = pl.multiple_of((position[0] ^ bit[0]) * count, count)
        for i in range(piece.shape[0]):
            high, low = split(piece[i])
            highs[bit[1] + i, pl.ds(row, count), :] = high
            lows[bit[1] + i, pl.ds(row, count), :] = low


def prepare(position, held, branches, channels):
    bits = list(held)
    shape = jax.ShapeDtypeStruct((branches, channels, channels), BF16)
    return pl.pallas_call(
        functools.partial(prepare_kernel, bits),
        out_shape=(shape, shape),
        in_specs=[SCALAR] + [WHOLE] * len(bits),
        out_specs=(WHOLE, WHOLE),
        compiler_params=pltpu.CompilerParams(vmem_limit_bytes=VMEM_LIMIT),
        cost_estimate=pl.CostEstimate(
            flops=0, bytes_accessed=8 * branches * channels * channels, transcendentals=0
        ),
    )(position, *[held[b] for b in bits])


def doubled(x, axis, bit, dim):
    other = swap(x, axis, bit)
    upper = (lax.axis_index(axis) & bit) != 0
    return jnp.where(
        upper, jnp.concatenate([other, x], dim), jnp.concatenate([x, other], dim)
    )


def gather_taps(taps, axis):
    size = lax.axis_size(axis)
    if size & (size - 1):
        return lax.all_gather(taps, axis, axis=2, tiled=True)
    bit = 1
    while bit < size:
        taps = doubled(taps, axis, bit, 2)
        bit *= 2
    return taps


def gather_matrices(shard, axis):
    size = lax.axis_size(axis)
    branches, _, channels = shard.shape
    position = lax.axis_index(axis)
    if size & (size - 1) or size < 8:
        shard = lax.all_gather(shard, axis, axis=1, tiled=True)
        return prepare(jnp.zeros((1,), jnp.int32), {(0, 0): shard}, branches, channels)
    bit = 8
    while bit < size:
        shard = doubled(shard, axis, bit, 1)
        bit *= 2
    x = swap(shard, axis, 2)
    y = swap(shard, axis, 4)
    core = swap(shard, axis, 1)
    half = branches // 2
    far_x = swap(y[:half], axis, 2)
    far_y = swap(x[half:], axis, 4)
    held = {
        (0, 0): shard,
        (1, 0): core,
        (2, 0): x,
        (3, 0): swap(x, axis, 1),
        (4, 0): y,
        (5, 0): swap(y, axis, 1),
        (6, 0): far_x,
        (7, 0): swap(far_x, axis, 1),
        (6, half): far_y,
        (7, half): swap(far_y, axis, 1),
    }
    if size > 8:
        upper = size // 8
        held = {
            k: v.reshape(v.shape[0] * upper, v.shape[1] // upper, channels)
            for k, v in held.items()
        }
        return prepare_blocks(position, held, branches, channels, upper)
    return prepare(position.reshape(1), held, branches, channels)


def prepare_blocks(position, held, branches, channels, upper):
    whole = jnp.zeros((branches, upper, 8, channels // (8 * upper), channels), F32)
    for (bit, first), piece in held.items():
        count = piece.shape[0] // upper
        piece = piece.reshape(count, upper, 1, piece.shape[1], channels)
        lower = (position & 7) ^ bit
        whole = lax.dynamic_update_slice(whole, piece, (first, 0, lower, 0, 0))
    whole = whole.reshape(branches, channels, channels)
    return prepare(jnp.zeros((1,), jnp.int32), {(0, 0): whole}, branches, channels)


def body(pair, stems, taps, matrices):
    section = lax.axis_index("section").astype(jnp.int32).reshape(1)
    stems = stems[:, 0]
    ticks = stems.shape[0] + 1
    earlier, newest = pair[0, 0, 0], pair[0, 1, 0]
    highs, lows = gather_matrices(matrices[0], "dp")
    taps = gather_taps(taps[0], "dp")
    weights = (taps, highs, lows)
    outputs = []
    for tick in range(ticks):
        last = tick == ticks - 1
        if not last:
            passed_on = from_behind(newest, "section", min(tick, 1))
        early = early_part(tick, section, stems, earlier, *weights)
        output = late_part(
            tick, section, stems, newest, early, *weights, past=outputs if last else ()
        )
        outputs.append(output)
        if not last:
            earlier = passed_on
            newest = from_behind(output, "section")
    return output[None, :, None]


def solution(mesh):
    placed = (
        P("section", None, "dp", None, None, None),
        P(None, "dp", None, None, None),
        P("section", None, None, "dp"),
        P("section", None, "dp", None),
    )
    return jax.shard_map(
        body,
        mesh=mesh,
        in_specs=placed,
        out_specs=P("section", None, "dp", None, None, None),
        check_vma=False,
    )
```

```python
import functools

import jax
import jax.numpy as jnp
from jax import lax
from jax.experimental import pallas as pl
from jax.experimental.pallas import tpu as pltpu
from jax.sharding import PartitionSpec as P

F32 = jnp.float32
BF16 = jnp.bfloat16
VMEM_LIMIT = 16 * 1024 * 1024
LANES = 128
TAP_ROWS = 16


def swap(x, axis, bit):
    size = lax.axis_size(axis)
    return lax.ppermute(x, axis, [(i, i ^ bit) for i in range(size)])


def from_behind(x, axis, first=0, around=False):
    size = lax.axis_size(axis)
    pairs = [(i, i + 1) for i in range(first, size - 1)]
    return lax.ppermute(x, axis, pairs + [(size - 1, 0)] * (around and size > 1))


def from_ahead(x, axis):
    return lax.ppermute(x, axis, [(i + 1, i) for i in range(lax.axis_size(axis) - 1)])


def after(x, *others):
    return lax.optimization_barrier((x, *others))[0]


def begin(source, target, sem):
    copy = pltpu.make_async_copy(source, target, sem)
    copy.start()
    return copy


def split(x):
    high = x.astype(BF16)
    return high, (x - high.astype(F32)).astype(BF16)


def call(kernel, outs, operands, scratch, copies, cost, apart=(), outs_apart=(), aliases=None, limit=VMEM_LIMIT):
    def spec(x, i, apart):
        space = pl.ANY if i in apart else pltpu.SMEM if x.dtype == jnp.int32 else pltpu.VMEM
        return pl.BlockSpec(memory_space=space)

    return pl.pallas_call(
        kernel,
        out_shape=outs,
        in_specs=[spec(x, i, apart) for i, x in enumerate(operands)],
        out_specs=tuple(spec(x, i, outs_apart) for i, x in enumerate(outs)),
        scratch_shapes=[pltpu.VMEM(*s) for s in scratch] + [pltpu.SemaphoreType.DMA((copies,))],
        input_output_aliases=aliases or {},
        compiler_params=pltpu.CompilerParams(vmem_limit_bytes=limit),
        cost_estimate=cost,
    )(*operands)


def cost(shape, convolutions):
    rows, columns, channels = shape
    size = rows * columns * channels
    return pl.CostEstimate(
        flops=6 * convolutions * size * channels,
        bytes_accessed=4 * (3 * size + convolutions * channels * channels),
        transcendentals=0,
    )


def shifted(u, by):
    side = u.shape[1]
    column = lax.broadcasted_iota(jnp.int32, u.shape, 1)
    outside = 0 if by == 1 else side - 1
    return jnp.where(column == outside, 0.0, pltpu.roll(u, by % side, 1))


def depthwise(source, table, branch, low, width):
    x = jnp.maximum(source[:, :, low : low + width], 0.0)
    nothing = jnp.zeros((1,) + x.shape[1:], F32)
    above = jnp.concatenate([nothing, x[:-1]], 0)
    below = jnp.concatenate([x[1:], nothing], 0)
    tap = [table[low // width, branch, k : k + 1, :].reshape(1, 1, width) for k in range(9)]
    by_column = [above * tap[j] + x * tap[3 + j] + below * tap[6 + j] for j in range(3)]
    return shifted(by_column[0], 1) + by_column[1] + shifted(by_column[2], -1)


def separable(source, table, highs, lows, branch):
    rows, columns, channels = source.shape
    width = min(LANES, channels)
    depth = min(256, channels)
    total = None
    for k in range(0, channels, depth):
        parts = []
        for low in range(k, k + depth, width):
            mixed_in = depthwise(source, table, branch, low, width)
            parts.append(split(mixed_in.reshape(rows * columns, width)))
        high = jnp.concatenate([p[0] for p in parts], 1)
        low = jnp.concatenate([p[1] for p in parts], 1)
        matrix_high = highs[branch, k : k + depth, :]
        matrix_low = lows[branch, k : k + depth, :]
        product = jnp.dot(high, matrix_high, preferred_element_type=F32)
        product = product + jnp.dot(low, matrix_high, preferred_element_type=F32)
        product = product + jnp.dot(high, matrix_low, preferred_element_type=F32)
        total = product if total is None else total + product
    return total.reshape(source.shape)


def fetch(tick, at, section, stems, got, held, sem):
    for s in range(at):

        @pl.when(section == s)
        def _(s=s):
            begin(stems.at[tick - 1 - s], held, sem)

    @pl.when(section >= at)
    def _():
        begin(got, held, sem)

    return pltpu.make_async_copy(got, held, sem)


def early_kernel(tick, section, stems, got, table, highs, lows, out, held, sem):
    fetch(tick, min(tick, 2), section[0], stems, got, held, sem.at[0]).wait()
    out[...] = separable(held, table, highs, lows, 1)


def late_kernel(tick, ticks, section, stems, got, early, table, highs, lows, past, *rest):
    outs, (newest, first, second, sem) = rest[-(6 if tick < ticks - 1 else 5) : -4], rest[-4:]
    emitted = outs[0]
    store = begin(past, emitted.at[tick - 1], sem.at[1])
    fetch(tick, min(tick, 1), section[0], stems, got, newest, sem.at[0]).wait()
    first[...] = separable(newest, table, highs, lows, 0) + early[...]
    second[...] = separable(first, table, highs, lows, 2) + newest[...]
    output = newest if tick == ticks - 1 else outs[1]
    output[...] = separable(second, table, highs, lows, 3) + first[...]
    store.wait()
    if tick == ticks - 1:
        begin(output, emitted.at[tick], sem.at[0]).wait()


def early_part(tick, section, stems, got, weights):
    shape = got.shape
    return call(
        functools.partial(early_kernel, tick),
        (jax.ShapeDtypeStruct(shape, F32),),
        (section, stems, got, *weights),
        [(shape, F32)],
        1,
        cost(shape, 1),
        apart=(1, 2),
    )[0]


def late_part(tick, ticks, section, stems, got, early, weights, past, emitted):
    shape = got.shape
    last = tick == ticks - 1
    whole = jax.ShapeDtypeStruct((ticks,) + shape, F32)
    operands = (section, stems, got, early, *weights, past)
    return call(
        functools.partial(late_kernel, tick, ticks),
        (whole,) if last else (whole, jax.ShapeDtypeStruct(shape, F32)),
        operands if emitted is None else operands + (emitted,),
        [(shape, F32)] * 3,
        2,
        cost(shape, 3),
        apart=(1, 2, 8),
        outs_apart=(0,),
        aliases=None if emitted is None else {8: 0},
    )


def join(key, lower, position, uppers, count, branches, block, highs, lows):
    for u in range(uppers):
        at = u * lower + ((position & (lower - 1)) ^ key)
        row = pl.multiple_of(at * count, count)
        for i in branches:
            high, low = split(block(u, i))
            highs[i, pl.ds(row, count), :] = high
            lows[i, pl.ds(row, count), :] = low


def near_kernel(keys, lower, position, *refs):
    pieces, (highs, lows, _) = refs[:-3], refs[-3:]
    for key, piece in zip(keys, pieces):
        uppers, branches, count, _ = piece.shape
        block = lambda u, i, piece=piece: piece[u, i]
        join(key, lower, position[0], uppers, count, range(branches), block, highs, lows)


def near_part(position, blocks, lower):
    uppers, branches, _, channels = blocks[0].shape
    matrices = jax.ShapeDtypeStruct((branches, channels, channels), BF16)
    return call(
        functools.partial(near_kernel, list(blocks), lower),
        (matrices, matrices),
        (position, *blocks.values()),
        [],
        1,
        pl.CostEstimate(flops=0, bytes_accessed=8 * matrices.size, transcendentals=0),
    )


def halves_kernel(x, y, *refs):
    taps, (one, two, sem) = refs[:-3], refs[-3:]
    uppers, branches, count, _ = x.shape
    half = branches // 2
    copies = []
    for u in range(uppers):
        for i in range(half):
            rows = pl.ds(i * count, count)
            n = 2 * (u * half + i)
            copies.append(begin(y.at[u, i], one.at[u, rows], sem.at[n]))
            copies.append(begin(x.at[u, half + i], two.at[u, rows], sem.at[n + 1]))
    for chip in taps:
        for out in (one, two):
            for n in range(branches):
                out[0, half * count : half * count + 9, n * LANES : (n + 1) * LANES] = chip[n]
    for copy in copies:
        copy.wait()


def halves(x, y, *taps):
    uppers, branches, count, channels = x.shape
    half = branches // 2
    out = jax.ShapeDtypeStruct((uppers, half * count + TAP_ROWS * len(taps), channels), F32)
    work = pl.CostEstimate(flops=0, bytes_accessed=4 * x.size, transcendentals=0)
    return call(halves_kernel, (out, out), (x, y, *taps), [], 2 * half * uppers, work)


def first_kernel(n_far, n_taps, lower, position, newest, pair, highs_in, lows_in, *refs):
    far, taps, refs = refs[:n_far], refs[n_far : n_far + n_taps], refs[n_far + n_taps :]
    out, highs, lows, table, earlier, first, second, sem = refs
    load = begin(pair.at[0], earlier, sem.at[0])
    branches, channels, _ = highs.shape
    half = branches // 2
    if n_taps == 1:
        table[...] = taps[0][...]
    else:
        chip = position[0] // 2
        for n in range(branches):
            table[chip, n] = taps[0][n]
            table[chip ^ 3, n] = taps[1][n]
            for j in (1, 2):
                block = far[2 * j - 2]
                row = block.shape[1] - TAP_ROWS
                table[chip ^ j, n] = block[0, row : row + 9, n * LANES : (n + 1) * LANES]
    for j, piece in enumerate(far):
        uppers = piece.shape[0]
        count = channels // (uppers * lower)
        which = range(half) if j < 2 else range(half, branches)

        def block(u, i, piece=piece, which=which, count=count):
            at = (i - which[0]) * count
            return piece[u, at : at + count, :]

        join(6 + j % 2, lower, position[0], uppers, count, which, block, highs, lows)
    first[...] = separable(newest, table, highs, lows, 0)
    load.wait()
    first[...] += separable(earlier, table, highs, lows, 1)
    second[...] = separable(first, table, highs, lows, 2) + newest[...]
    out[...] = separable(second, table, highs, lows, 3) + first[...]


def first_part(position, newest, pair, matrices, far, lower, taps):
    shape, channels = newest.shape, newest.shape[-1]
    branches = matrices[0].shape[0]
    lanes = min(LANES, channels)
    like = [jax.ShapeDtypeStruct(m.shape, m.dtype) for m in matrices]
    return call(
        functools.partial(first_kernel, len(far), len(taps), lower),
        (
            jax.ShapeDtypeStruct(shape, F32),
            *like,
            jax.ShapeDtypeStruct((channels // lanes, branches, 9, lanes), F32),
        ),
        (position, newest, pair, *matrices, *far, *taps),
        [(shape, F32)] * 3,
        1,
        cost(shape, 4),
        apart=(2,),
        aliases={3: 1, 4: 2},
    )


def doubled(x, axis, bit, dim):
    other = swap(x, axis, bit)
    upper = (lax.axis_index(axis) & bit) != 0
    return jnp.where(upper, jnp.concatenate([other, x], dim), jnp.concatenate([x, other], dim))


def near_taps(taps, axis):
    size = lax.axis_size(axis)
    branches, count, width = taps.shape
    if size == 8 and 2 * width == LANES:
        chip = doubled(taps, axis, 1, 2)
        return chip, swap(chip, axis, 6)
    if size & (size - 1):
        taps = lax.all_gather(taps, axis, axis=2, tiled=True)
    else:
        bit = 1
        while bit < size:
            taps = doubled(taps, axis, bit, 2)
            bit *= 2
    channels = taps.shape[-1]
    lanes = min(LANES, channels)
    taps = taps.reshape(branches, count, channels // lanes, lanes)
    return (taps.transpose(2, 0, 1, 3),)


def from_neighbours(shard, axis):
    shard = shard[None]
    bit = 8
    while bit < lax.axis_size(axis):
        shard = doubled(shard, axis, bit, 0)
        bit *= 2
    return shard, swap(shard, axis, 2), swap(shard, axis, 4)


def body(pair, stems, taps, matrices):
    section = lax.axis_index("section").astype(jnp.int32).reshape(1)
    position = lax.axis_index("dp").astype(jnp.int32).reshape(1)
    stems = stems[:, 0]
    ticks = stems.shape[0] + 1
    pair = pair[0, :, 0]
    newest = pair[1]
    size = lax.axis_size("dp")
    taps = near_taps(after(taps[0], section, position), "dp")
    passed_on = from_behind(after(newest, taps[0]), "section", around=True)
    if size & (size - 1) or size < 8:
        lower, far = 1, ()
        partial = near_part(position, {0: lax.all_gather(matrices[0], "dp")}, lower)
    else:
        lower = 8
        own, x, y = from_neighbours(matrices[0], "dp")
        near = {0: own, 1: swap(own, "dp", 1), 2: x, 4: y}
        one, two = halves(after(x, near[1], *taps), y, *taps[: len(taps) - 1])
        x_late, y_late, *_ = lax.optimization_barrier((x, y, one, two))
        near.update({3: swap(x_late, "dp", 1), 5: swap(y_late, "dp", 1)})
        one, two = swap(one, "dp", 2), swap(two, "dp", 4)
        partial = near_part(after(position, passed_on), near, lower)
        one, two, *_ = lax.optimization_barrier((one, two, *partial))
        far = (one, swap(one, "dp", 1), two, swap(two, "dp", 1))
    output, *weights, table = first_part(position, newest, pair, partial, far, lower, taps)
    weights = (table, *weights)
    emitted = None
    for tick in range(1, ticks):
        earlier, newest, past = passed_on, from_behind(output, "section"), output
        if tick < ticks - 1:
            passed_on = from_behind(newest, "section", 1)
        early = early_part(tick, section, stems, earlier, weights)
        emitted, *output = late_part(
            tick, ticks, section, stems, newest, early, weights, past, emitted
        )
        output = output[0] if output else None
    return emitted[None, :, None]


def solution(mesh):
    placed = (
        P("section", None, "dp", None, None, None),
        P(None, "dp", None, None, None),
        P("section", None, None, "dp"),
        P("section", None, "dp", None),
    )
    return jax.shard_map(
        body,
        mesh=mesh,
        in_specs=placed,
        out_specs=P("section", None, "dp", None, None, None),
        check_vma=False,
    )
```

```python
import functools

import jax
import jax.numpy as jnp
from jax import lax
from jax.experimental import pallas as pl
from jax.experimental.pallas import tpu as pltpu
from jax.sharding import PartitionSpec as P

F32 = jnp.float32
BF16 = jnp.bfloat16
VMEM_LIMIT = 16 * 1024 * 1024
LANES = 128
TAP_ROWS = 16


def swap(x, axis, bit):
    size = lax.axis_size(axis)
    return lax.ppermute(x, axis, [(i, i ^ bit) for i in range(size)])


def from_behind(x, axis, first=0, around=False):
    size = lax.axis_size(axis)
    pairs = [(i, i + 1) for i in range(first, size - 1)]
    return lax.ppermute(x, axis, pairs + [(size - 1, 0)] * (around and size > 1))


def from_ahead(x, axis):
    return lax.ppermute(x, axis, [(i + 1, i) for i in range(lax.axis_size(axis) - 1)])


def after(x, *others):
    return lax.optimization_barrier((x, *others))[0]


def begin(source, target, sem):
    copy = pltpu.make_async_copy(source, target, sem)
    copy.start()
    return copy


def split(x):
    high = x.astype(BF16)
    return high, (x - high.astype(F32)).astype(BF16)


def call(kernel, outs, operands, scratch, copies, cost, apart=(), outs_apart=(), aliases=None, limit=VMEM_LIMIT):
    def spec(x, i, apart):
        space = pl.ANY if i in apart else pltpu.SMEM if x.dtype == jnp.int32 else pltpu.VMEM
        return pl.BlockSpec(memory_space=space)

    return pl.pallas_call(
        kernel,
        out_shape=outs,
        in_specs=[spec(x, i, apart) for i, x in enumerate(operands)],
        out_specs=tuple(spec(x, i, outs_apart) for i, x in enumerate(outs)),
        scratch_shapes=[pltpu.VMEM(*s) for s in scratch] + [pltpu.SemaphoreType.DMA((copies,))],
        input_output_aliases=aliases or {},
        compiler_params=pltpu.CompilerParams(vmem_limit_bytes=limit),
        cost_estimate=cost,
    )(*operands)


def cost(shape, convolutions):
    rows, columns, channels = shape
    size = rows * columns * channels
    return pl.CostEstimate(
        flops=6 * convolutions * size * channels,
        bytes_accessed=4 * (3 * size + convolutions * channels * channels),
        transcendentals=0,
    )


def shifted(u, by):
    side = u.shape[1]
    column = lax.broadcasted_iota(jnp.int32, u.shape, 1)
    outside = 0 if by == 1 else side - 1
    return jnp.where(column == outside, 0.0, pltpu.roll(u, by % side, 1))


def depthwise(source, table, branch, low, width):
    x = jnp.maximum(source[:, :, low : low + width], 0.0)
    nothing = jnp.zeros((1,) + x.shape[1:], F32)
    above = jnp.concatenate([nothing, x[:-1]], 0)
    below = jnp.concatenate([x[1:], nothing], 0)
    tap = [table[low // width, branch, k : k + 1, :].reshape(1, 1, width) for k in range(9)]
    by_column = [above * tap[j] + x * tap[3 + j] + below * tap[6 + j] for j in range(3)]
    return shifted(by_column[0], 1) + by_column[1] + shifted(by_column[2], -1)


def separable(source, table, highs, lows, branch):
    rows, columns, channels = source.shape
    width = min(LANES, channels)
    depth = min(256, channels)
    total = None
    for k in range(0, channels, depth):
        parts = []
        for low in range(k, k + depth, width):
            mixed_in = depthwise(source, table, branch, low, width)
            parts.append(split(mixed_in.reshape(rows * columns, width)))
        high = jnp.concatenate([p[0] for p in parts], 1)
        low = jnp.concatenate([p[1] for p in parts], 1)
        matrix_high = highs[branch, k : k + depth, :]
        matrix_low = lows[branch, k : k + depth, :]
        product = jnp.dot(high, matrix_high, preferred_element_type=F32)
        product = product + jnp.dot(low, matrix_high, preferred_element_type=F32)
        product = product + jnp.dot(high, matrix_low, preferred_element_type=F32)
        total = product if total is None else total + product
    return total.reshape(source.shape)


def fetch(tick, at, section, stems, got, held, sem):
    for s in range(at):

        @pl.when(section == s)
        def _(s=s):
            begin(stems.at[tick - 1 - s], held, sem)

    @pl.when(section >= at)
    def _():
        begin(got, held, sem)

    return pltpu.make_async_copy(got, held, sem)


def early_kernel(tick, at, section, stems, got, table, highs, lows, out, held, sem):
    fetch(tick, at, section[0], stems, got, held, sem.at[0]).wait()
    out[...] = separable(held, table, highs, lows, 1)


def late_kernel(tick, at, section, stems, got, early, table, highs, lows, past, *rest):
    emitted, out, newest, first, second, sem = rest[-6:]
    store = begin(past, emitted.at[tick - 1], sem.at[1])
    fetch(tick, at, section[0], stems, got, newest, sem.at[0]).wait()
    first[...] = separable(newest, table, highs, lows, 0) + early[...]
    second[...] = separable(first, table, highs, lows, 2) + newest[...]
    out[...] = separable(second, table, highs, lows, 3) + first[...]
    store.wait()


def early_part(tick, at, section, stems, got, weights):
    shape = got.shape
    return call(
        functools.partial(early_kernel, tick, at),
        (jax.ShapeDtypeStruct(shape, F32),),
        (section, stems, got, *weights),
        [(shape, F32)],
        1,
        cost(shape, 1),
        apart=(1, 2),
    )[0]


def late_part(tick, at, section, stems, got, early, weights, past, emitted, weight=2):
    shape = got.shape
    whole = jax.ShapeDtypeStruct((stems.shape[0] + 1,) + shape, F32)
    operands = (section, stems, got, early, *weights, past)
    return call(
        functools.partial(late_kernel, tick, at),
        (whole, jax.ShapeDtypeStruct(shape, F32)),
        operands if emitted is None else operands + (emitted,),
        [(shape, F32)] * 3,
        2,
        cost(shape, 3 * weight),
        apart=(1, 2, 8),
        outs_apart=(0,),
        aliases=None if emitted is None else {8: 0},
    )


def stem_kernel(stems, table, highs, lows, out, held, first, second, sem):
    begin(stems.at[stems.shape[0] - 1], held, sem.at[0]).wait()
    first[...] = separable(held, table, highs, lows, 0)
    first[...] += separable(held, table, highs, lows, 1)
    second[...] = separable(first, table, highs, lows, 2) + held[...]
    out[...] = separable(second, table, highs, lows, 3) + first[...]


def stem_part(stems, weights):
    shape = stems.shape[1:]
    a_map = jax.ShapeDtypeStruct(shape, F32)
    scratch = [(shape, F32)] * 3
    operands = (stems, *weights)
    return call(stem_kernel, (a_map,), operands, scratch, 1, cost(shape, 4), apart=(0,))[0]


def last_kernel(section, got, own, _, emitted, sem):
    target = emitted.at[emitted.shape[0] - 1]

    @pl.when(section[0] == 0)
    def _():
        begin(own, target, sem.at[0])

    @pl.when(section[0] > 0)
    def _():
        begin(got, target, sem.at[0])

    pltpu.make_async_copy(got, target, sem.at[0]).wait()


def last_part(section, got, own, emitted):
    whole = jax.ShapeDtypeStruct(emitted.shape, F32)
    work = pl.CostEstimate(flops=0, bytes_accessed=8 * got.size, transcendentals=0)
    operands = (section, got, own, emitted)
    return call(
        last_kernel, (whole,), operands, [], 1, work, apart=(3,), outs_apart=(0,), aliases={3: 0}
    )[0]


def join(key, lower, position, uppers, count, branches, block, highs, lows):
    for u in range(uppers):
        at = u * lower + ((position & (lower - 1)) ^ key)
        row = pl.multiple_of(at * count, count)
        for i in branches:
            high, low = split(block(u, i))
            highs[i, pl.ds(row, count), :] = high
            lows[i, pl.ds(row, count), :] = low


def near_kernel(keys, lower, position, *refs):
    pieces, (highs, lows, _) = refs[:-3], refs[-3:]
    for key, piece in zip(keys, pieces):
        uppers, branches, count, _ = piece.shape
        block = lambda u, i, piece=piece: piece[u, i]
        join(key, lower, position[0], uppers, count, range(branches), block, highs, lows)


def near_part(position, blocks, lower):
    uppers, branches, _, channels = blocks[0].shape
    matrices = jax.ShapeDtypeStruct((branches, channels, channels), BF16)
    return call(
        functools.partial(near_kernel, list(blocks), lower),
        (matrices, matrices),
        (position, *blocks.values()),
        [],
        1,
        pl.CostEstimate(flops=0, bytes_accessed=8 * matrices.size, transcendentals=0),
    )


def halves_kernel(x, y, *refs):
    taps, (one, two, sem) = refs[:-3], refs[-3:]
    uppers, branches, count, _ = x.shape
    half = branches // 2
    copies = []
    for u in range(uppers):
        for i in range(half):
            rows = pl.ds(i * count, count)
            n = 2 * (u * half + i)
            copies.append(begin(y.at[u, i], one.at[u, rows], sem.at[n]))
            copies.append(begin(x.at[u, half + i], two.at[u, rows], sem.at[n + 1]))
    for chip in taps:
        for out in (one, two):
            for n in range(branches):
                out[0, half * count : half * count + 9, n * LANES : (n + 1) * LANES] = chip[n]
    for copy in copies:
        copy.wait()


def halves(x, y, *taps):
    uppers, branches, count, channels = x.shape
    half = branches // 2
    out = jax.ShapeDtypeStruct((uppers, half * count + TAP_ROWS * len(taps), channels), F32)
    work = pl.CostEstimate(flops=0, bytes_accessed=4 * x.size, transcendentals=0)
    return call(halves_kernel, (out, out), (x, y, *taps), [], 2 * half * uppers, work)


def join_far(far, lower, position, highs, lows):
    branches, channels, _ = highs.shape
    half = branches // 2
    for j, piece in enumerate(far):
        uppers = piece.shape[0]
        count = channels // (uppers * lower)
        which = range(half) if j < 2 else range(half, branches)

        def block(u, i, piece=piece, which=which, count=count):
            at = (i - which[0]) * count
            return piece[u, at : at + count, :]

        join(6 + j % 2, lower, position, uppers, count, which, block, highs, lows)


def stack_kernel(*refs):
    pieces, (out, sem) = refs[:-2], refs[-2:]
    copies = [begin(piece, out.at[i], sem.at[i]) for i, piece in enumerate(pieces)]
    for copy in copies:
        copy.wait()


def stack(*pieces):
    n = len(pieces)
    out = jax.ShapeDtypeStruct((n,) + pieces[0].shape, F32)
    work = pl.CostEstimate(flops=0, bytes_accessed=8 * n * pieces[0].size, transcendentals=0)
    return call(stack_kernel, (out,), pieces, [], n, work, apart=range(n))[0]


def pack_kernel(one, two, table, out, sem):
    parts, branches, count, lanes = table.shape
    rows = (out.shape[1] - branches * TAP_ROWS) // 2
    copies = []
    for i, piece in enumerate((one, two)):
        source = piece.at[:, pl.ds(0, rows)]
        copies.append(begin(source, out.at[:, pl.ds(i * rows, rows)], sem.at[i]))
    for n in range(branches):
        row = 2 * rows + n * TAP_ROWS
        for p in range(parts):
            out[0, row : row + count, p * lanes : (p + 1) * lanes] = table[p, n]
    for copy in copies:
        copy.wait()


def pack(one, two, table, rows):
    uppers, _, channels = one.shape
    out = jax.ShapeDtypeStruct((uppers, 2 * rows + table.shape[1] * TAP_ROWS, channels), F32)
    work = pl.CostEstimate(flops=0, bytes_accessed=16 * one.size, transcendentals=0)
    return call(pack_kernel, (out,), (one, two, table), [], 2, work)[0]


def next_kernel(lower, position, near, near_core, far, far_core, highs, lows, table, _):
    branches, channels, _ = highs.shape
    _, uppers, _, count, _ = near.shape
    for core, (near_blocks, far_blocks) in enumerate(((near, far), (near_core, far_core))):
        for j in range(3):
            block = lambda u, i: near_blocks[j, u, i]
            join(2 * j + core, lower, position[0], uppers, count, range(branches), block, highs, lows)
        block = lambda u, i: far_blocks[u, i * count : (i + 1) * count, :]
        join(6 + core, lower, position[0], uppers, count, range(branches), block, highs, lows)
    parts, _, taps, lanes = table.shape
    for n in range(branches):
        row = branches * count + n * TAP_ROWS
        for p in range(parts):
            table[p, n] = far[0, row : row + taps, p * lanes : (p + 1) * lanes]


def next_part(position, near, near_core, far, far_core, like, lower):
    table, highs, lows = (jax.ShapeDtypeStruct(w.shape, w.dtype) for w in like)
    work = pl.CostEstimate(flops=0, bytes_accessed=16 * near.size, transcendentals=0)
    operands = (position, near, near_core, far, far_core)
    kernel = functools.partial(next_kernel, lower)
    highs, lows, table = call(kernel, (highs, lows, table), operands, [], 1, work)
    return table, highs, lows


def first_kernel(n_far, n_taps, lower, position, newest, pair, highs_in, lows_in, *refs):
    far, taps, refs = refs[:n_far], refs[n_far : n_far + n_taps], refs[n_far + n_taps :]
    out, highs, lows, table, earlier, first, second, sem = refs
    load = begin(pair.at[0], earlier, sem.at[0])
    branches, channels, _ = highs.shape
    half = branches // 2
    if n_taps == 1:
        table[...] = taps[0][...]
    else:
        chip = position[0] // 2
        for n in range(branches):
            table[chip, n] = taps[0][n]
            table[chip ^ 3, n] = taps[1][n]
            for j in (1, 2):
                block = far[2 * j - 2]
                row = block.shape[1] - TAP_ROWS
                table[chip ^ j, n] = block[0, row : row + 9, n * LANES : (n + 1) * LANES]
    join_far(far, lower, position[0], highs, lows)
    first[...] = separable(newest, table, highs, lows, 0)
    load.wait()
    first[...] += separable(earlier, table, highs, lows, 1)
    second[...] = separable(first, table, highs, lows, 2) + newest[...]
    out[...] = separable(second, table, highs, lows, 3) + first[...]


def first_part(position, newest, pair, matrices, far, lower, taps):
    shape, channels = newest.shape, newest.shape[-1]
    branches = matrices[0].shape[0]
    lanes = min(LANES, channels)
    like = [jax.ShapeDtypeStruct(m.shape, m.dtype) for m in matrices]
    return call(
        functools.partial(first_kernel, len(far), len(taps), lower),
        (
            jax.ShapeDtypeStruct(shape, F32),
            *like,
            jax.ShapeDtypeStruct((channels // lanes, branches, 9, lanes), F32),
        ),
        (position, newest, pair, *matrices, *far, *taps),
        [(shape, F32)] * 3,
        1,
        cost(shape, 4),
        apart=(2,),
        aliases={3: 1, 4: 2},
    )


def doubled(x, axis, bit, dim):
    other = swap(x, axis, bit)
    upper = (lax.axis_index(axis) & bit) != 0
    return jnp.where(upper, jnp.concatenate([other, x], dim), jnp.concatenate([x, other], dim))


def near_taps(taps, axis):
    size = lax.axis_size(axis)
    branches, count, width = taps.shape
    if size == 8 and 2 * width == LANES:
        chip = doubled(taps, axis, 1, 2)
        return chip, swap(chip, axis, 6)
    if size & (size - 1):
        taps = lax.all_gather(taps, axis, axis=2, tiled=True)
    else:
        bit = 1
        while bit < size:
            taps = doubled(taps, axis, bit, 2)
            bit *= 2
    channels = taps.shape[-1]
    lanes = min(LANES, channels)
    taps = taps.reshape(branches, count, channels // lanes, lanes)
    return (taps.transpose(2, 0, 1, 3),)


def from_neighbours(shard, axis):
    shard = shard[None]
    bit = 8
    while bit < lax.axis_size(axis):
        shard = doubled(shard, axis, bit, 0)
        bit *= 2
    return shard, swap(shard, axis, 2), swap(shard, axis, 4)


def body(pair, stems, taps, matrices):
    section = lax.axis_index("section").astype(jnp.int32).reshape(1)
    position = lax.axis_index("dp").astype(jnp.int32).reshape(1)
    stems = stems[:, 0]
    ticks = stems.shape[0] + 1
    pair = pair[0, :, 0]
    shard = matrices[0]
    newest = pair[1]
    size = lax.axis_size("dp")
    simple = size & (size - 1) or size < 8
    lower = 1 if simple else 8
    taps = near_taps(after(taps[0], section, position), "dp")
    passed_on = from_behind(after(newest, taps[0]), "section", around=True)
    far = ()
    if simple:
        partial = near_part(position, {0: lax.all_gather(shard, "dp")}, lower)
    else:
        own, x, y = from_neighbours(shard, "dp")
        near = {0: own, 1: swap(own, "dp", 1), 2: x, 4: y}
        one, two = halves(after(x, near[1], *taps), y, *taps[: len(taps) - 1])
        x_late, y_late, *_ = lax.optimization_barrier((x, y, one, two))
        near.update({3: swap(x_late, "dp", 1), 5: swap(y_late, "dp", 1)})
        one, two = swap(one, "dp", 2), swap(two, "dp", 4)
        partial = near_part(after(position, passed_on), near, lower)
        one, two, *_ = lax.optimization_barrier((one, two, *partial))
        far = (one, swap(one, "dp", 1), two, swap(two, "dp", 1))
    output, *weights, table = first_part(position, newest, pair, partial, far, lower, taps)
    weights = (table, *weights)

    if simple:
        next_shard = lax.all_gather(from_ahead(shard, "section"), "dp")
        next_weights = (from_ahead(table, "section"), *near_part(position, {0: next_shard}, lower))
    else:
        near = lax.optimization_barrier((own, x, y, *partial))[:3]
        next_near = from_ahead(stack(*near), "section")
        rows = far[0].shape[1] - TAP_ROWS * (len(taps) - 1)
    emitted = None
    held = (1, 0, newest)
    for tick in range(1, ticks - 1):
        earlier, newest, past = passed_on, from_behind(output, "section"), output
        if tick > 1:
            earlier = after(earlier, output)
        passed_on = from_behind(newest, "section", 1)
        early = early_part(tick, min(tick, 2), section, stems, earlier, weights)
        if tick == 1 and not simple:
            next_far = from_ahead(pack(after(far[0], early), far[2], table, rows), "section")
        emitted, output = late_part(
            tick, 1, section, stems, newest, early, weights, past, emitted, 12 if tick > 1 else 2
        )
        held = (tick, 1, newest)
        last_early = early

    if not simple:
        next_near, next_far, _ = lax.optimization_barrier((next_near, next_far, last_early))
        blocks = next_near, swap(next_near, "dp", 1), next_far, swap(next_far, "dp", 1)
        next_weights = next_part(position, *blocks, weights, lower)
    early = early_part(held[0], held[1], section, stems, held[2], next_weights)
    emitted, ahead = late_part(
        ticks - 1, 0, section, stems, output, early, next_weights, output, emitted
    )
    got = from_behind(ahead, "section")
    emitted = last_part(section, got, stem_part(stems, weights), emitted)
    return emitted[None, :, None]


def solution(mesh):
    placed = (
        P("section", None, "dp", None, None, None),
        P(None, "dp", None, None, None),
        P("section", None, None, "dp"),
        P("section", None, "dp", None),
    )
    return jax.shard_map(
        body,
        mesh=mesh,
        in_specs=placed,
        out_specs=P("section", None, "dp", None, None, None),
        check_vma=False,
    )
```

```python
import functools

import jax
import jax.numpy as jnp
from jax import lax
from jax.experimental import pallas as pl
from jax.experimental.pallas import tpu as pltpu
from jax.sharding import PartitionSpec as P

F32 = jnp.float32
BF16 = jnp.bfloat16
VMEM_LIMIT = 16 * 1024 * 1024
LANES = 128
TAP_ROWS = 16


def swap(x, axis, bit):
    size = lax.axis_size(axis)
    return lax.ppermute(x, axis, [(i, i ^ bit) for i in range(size)])


def from_behind(x, axis, first=0, around=False):
    size = lax.axis_size(axis)
    pairs = [(i, i + 1) for i in range(first, size - 1)]
    return lax.ppermute(x, axis, pairs + [(size - 1, 0)] * (around and size > 1))


def from_ahead(x, axis):
    return lax.ppermute(x, axis, [(i + 1, i) for i in range(lax.axis_size(axis) - 1)])


def after(x, *others):
    return lax.optimization_barrier((x, *others))[0]


def begin(source, target, sem):
    copy = pltpu.make_async_copy(source, target, sem)
    copy.start()
    return copy


def split(x):
    high = x.astype(BF16)
    return high, (x - high.astype(F32)).astype(BF16)


def call(kernel, outs, operands, scratch, copies, cost, apart=(), outs_apart=(), aliases=None, limit=VMEM_LIMIT):
    def spec(x, i, apart):
        space = pl.ANY if i in apart else pltpu.SMEM if x.dtype == jnp.int32 else pltpu.VMEM
        return pl.BlockSpec(memory_space=space)

    return pl.pallas_call(
        kernel,
        out_shape=outs,
        in_specs=[spec(x, i, apart) for i, x in enumerate(operands)],
        out_specs=tuple(spec(x, i, outs_apart) for i, x in enumerate(outs)),
        scratch_shapes=[pltpu.VMEM(*s) for s in scratch] + [pltpu.SemaphoreType.DMA((copies,))],
        input_output_aliases=aliases or {},
        compiler_params=pltpu.CompilerParams(vmem_limit_bytes=limit),
        cost_estimate=cost,
    )(*operands)


def cost(shape, convolutions):
    rows, columns, channels = shape
    size = rows * columns * channels
    return pl.CostEstimate(
        flops=6 * convolutions * size * channels,
        bytes_accessed=4 * (3 * size + convolutions * channels * channels),
        transcendentals=0,
    )


def shifted(u, by):
    side = u.shape[1]
    column = lax.broadcasted_iota(jnp.int32, u.shape, 1)
    outside = 0 if by == 1 else side - 1
    return jnp.where(column == outside, 0.0, pltpu.roll(u, by % side, 1))


def depthwise(source, table, branch, low, width):
    x = jnp.maximum(source[:, :, low : low + width], 0.0)
    nothing = jnp.zeros((1,) + x.shape[1:], F32)
    above = jnp.concatenate([nothing, x[:-1]], 0)
    below = jnp.concatenate([x[1:], nothing], 0)
    tap = [table[low // width, branch, k : k + 1, :].reshape(1, 1, width) for k in range(9)]
    by_column = [above * tap[j] + x * tap[3 + j] + below * tap[6 + j] for j in range(3)]
    return shifted(by_column[0], 1) + by_column[1] + shifted(by_column[2], -1)


def separable(source, table, highs, lows, branch):
    rows, columns, channels = source.shape
    width = min(LANES, channels)
    depth = min(256, channels)
    total = None
    for k in range(0, channels, depth):
        parts = []
        for low in range(k, k + depth, width):
            mixed_in = depthwise(source, table, branch, low, width)
            parts.append(split(mixed_in.reshape(rows * columns, width)))
        high = jnp.concatenate([p[0] for p in parts], 1)
        low = jnp.concatenate([p[1] for p in parts], 1)
        matrix_high = highs[branch, k : k + depth, :]
        matrix_low = lows[branch, k : k + depth, :]
        both = jnp.concatenate([high, low], 0)
        product = jnp.dot(both, matrix_high, preferred_element_type=F32)
        product = product[: high.shape[0]] + product[high.shape[0] :]
        product = product + jnp.dot(high, matrix_low, preferred_element_type=F32)
        total = product if total is None else total + product
    return total.reshape(source.shape)


def fetch(tick, at, section, stems, got, held, sem):
    for s in range(at):

        @pl.when(section == s)
        def _(s=s):
            begin(stems.at[tick - 1 - s], held, sem)

    @pl.when(section >= at)
    def _():
        begin(got, held, sem)

    return pltpu.make_async_copy(got, held, sem)


def early_kernel(tick, at, section, stems, got, table, highs, lows, out, held, sem):
    fetch(tick, at, section[0], stems, got, held, sem.at[0]).wait()
    out[...] = separable(held, table, highs, lows, 1)


def late_kernel(tick, at, section, stems, got, early, table, highs, lows, past, *rest):
    emitted, out, newest, first, second, sem = rest[-6:]
    store = begin(past, emitted.at[tick - 1], sem.at[1])
    fetch(tick, at, section[0], stems, got, newest, sem.at[0]).wait()
    first[...] = separable(newest, table, highs, lows, 0) + early[...]
    second[...] = separable(first, table, highs, lows, 2) + newest[...]
    out[...] = separable(second, table, highs, lows, 3) + first[...]
    store.wait()


def early_part(tick, at, section, stems, got, weights):
    shape = got.shape
    return call(
        functools.partial(early_kernel, tick, at),
        (jax.ShapeDtypeStruct(shape, F32),),
        (section, stems, got, *weights),
        [(shape, F32)],
        1,
        cost(shape, 1),
        apart=(1, 2),
    )[0]


def late_part(tick, at, section, stems, got, early, weights, past, emitted, weight=2):
    shape = got.shape
    whole = jax.ShapeDtypeStruct((stems.shape[0] + 1,) + shape, F32)
    operands = (section, stems, got, early, *weights, past)
    return call(
        functools.partial(late_kernel, tick, at),
        (whole, jax.ShapeDtypeStruct(shape, F32)),
        operands if emitted is None else operands + (emitted,),
        [(shape, F32)] * 3,
        2,
        cost(shape, 3 * weight),
        apart=(1, 2, 8),
        outs_apart=(0,),
        aliases=None if emitted is None else {8: 0},
    )


def stem_kernel(stems, table, highs, lows, out, held, first, second, sem):
    begin(stems.at[stems.shape[0] - 1], held, sem.at[0]).wait()
    first[...] = separable(held, table, highs, lows, 0)
    first[...] += separable(held, table, highs, lows, 1)
    second[...] = separable(first, table, highs, lows, 2) + held[...]
    out[...] = separable(second, table, highs, lows, 3) + first[...]


def stem_part(stems, weights):
    shape = stems.shape[1:]
    a_map = jax.ShapeDtypeStruct(shape, F32)
    scratch = [(shape, F32)] * 3
    operands = (stems, *weights)
    return call(stem_kernel, (a_map,), operands, scratch, 1, cost(shape, 4), apart=(0,))[0]


def last_kernel(section, got, own, _, emitted, sem):
    target = emitted.at[emitted.shape[0] - 1]

    @pl.when(section[0] == 0)
    def _():
        begin(own, target, sem.at[0])

    @pl.when(section[0] > 0)
    def _():
        begin(got, target, sem.at[0])

    pltpu.make_async_copy(got, target, sem.at[0]).wait()


def last_part(section, got, own, emitted):
    whole = jax.ShapeDtypeStruct(emitted.shape, F32)
    work = pl.CostEstimate(flops=0, bytes_accessed=8 * got.size, transcendentals=0)
    operands = (section, got, own, emitted)
    return call(
        last_kernel, (whole,), operands, [], 1, work, apart=(3,), outs_apart=(0,), aliases={3: 0}
    )[0]


def join(key, lower, position, uppers, count, branches, block, highs, lows):
    for u in range(uppers):
        at = u * lower + ((position & (lower - 1)) ^ key)
        row = pl.multiple_of(at * count, count)
        for i in branches:
            high, low = split(block(u, i))
            highs[i, pl.ds(row, count), :] = high
            lows[i, pl.ds(row, count), :] = low


def near_kernel(keys, lower, position, *refs):
    pieces, (highs, lows, _) = refs[:-3], refs[-3:]
    for key, piece in zip(keys, pieces):
        uppers, branches, count, _ = piece.shape
        block = lambda u, i, piece=piece: piece[u, i]
        join(key, lower, position[0], uppers, count, range(branches), block, highs, lows)


def near_part(position, blocks, lower):
    uppers, branches, _, channels = blocks[0].shape
    matrices = jax.ShapeDtypeStruct((branches, channels, channels), BF16)
    return call(
        functools.partial(near_kernel, list(blocks), lower),
        (matrices, matrices),
        (position, *blocks.values()),
        [],
        1,
        pl.CostEstimate(flops=0, bytes_accessed=8 * matrices.size, transcendentals=0),
    )


def half_kernel(start, block, *refs):
    taps, (out, sem) = refs[:-2], refs[-2:]
    uppers, branches, count, _ = block.shape
    half = branches // 2
    copies = []
    for u in range(uppers):
        for i in range(half):
            target = out.at[u, pl.ds(i * count, count)]
            copies.append(begin(block.at[u, start + i], target, sem.at[u * half + i]))
    for j, chip in enumerate(taps):
        row = half * count + j * TAP_ROWS
        for n in range(branches):
            out[0, row : row + 9, n * LANES : (n + 1) * LANES] = chip[n]
    for copy in copies:
        copy.wait()


def half_of(block, start, *taps):
    uppers, branches, count, channels = block.shape
    half = branches // 2
    out = jax.ShapeDtypeStruct((uppers, half * count + TAP_ROWS * len(taps), channels), F32)
    work = pl.CostEstimate(flops=0, bytes_accessed=4 * block.size, transcendentals=0)
    kernel = functools.partial(half_kernel, start * half)
    return call(kernel, (out,), (block, *taps), [], half * uppers, work)[0]


def join_far(far, lower, position, highs, lows):
    branches, channels, _ = highs.shape
    half = branches // 2
    for j, piece in enumerate(far):
        uppers = piece.shape[0]
        count = channels // (uppers * lower)
        which = range(half) if j < 2 else range(half, branches)

        def block(u, i, piece=piece, which=which, count=count):
            at = (i - which[0]) * count
            return piece[u, at : at + count, :]

        join(6 + j % 2, lower, position, uppers, count, which, block, highs, lows)


def stack_kernel(*refs):
    pieces, (out, sem) = refs[:-2], refs[-2:]
    copies = [begin(piece, out.at[i], sem.at[i]) for i, piece in enumerate(pieces)]
    for copy in copies:
        copy.wait()


def stack(*pieces):
    n = len(pieces)
    out = jax.ShapeDtypeStruct((n,) + pieces[0].shape, F32)
    work = pl.CostEstimate(flops=0, bytes_accessed=8 * n * pieces[0].size, transcendentals=0)
    return call(stack_kernel, (out,), pieces, [], n, work, apart=range(n))[0]


def table_rows(table):
    return -(-table.shape[1] * table.shape[2] // 8) * 8


def pack_kernel(one, two, table, out, sem):
    parts, branches, count, lanes = table.shape
    rows = (out.shape[1] - table_rows(table)) // 2
    copies = []
    for i, piece in enumerate((one, two)):
        source = piece.at[:, pl.ds(0, rows)]
        copies.append(begin(source, out.at[:, pl.ds(i * rows, rows)], sem.at[i]))
    for n in range(branches):
        row = 2 * rows + n * count
        for p in range(parts):
            out[0, row : row + count, p * lanes : (p + 1) * lanes] = table[p, n]
    for copy in copies:
        copy.wait()


def pack(one, two, table, rows):
    uppers, _, channels = one.shape
    out = jax.ShapeDtypeStruct((uppers, 2 * rows + table_rows(table), channels), F32)
    work = pl.CostEstimate(flops=0, bytes_accessed=16 * one.size, transcendentals=0)
    return call(pack_kernel, (out,), (one, two, table), [], 2, work)[0]


def next_kernel(lower, position, near, near_core, far, far_core, highs, lows, table, _):
    branches, channels, _ = highs.shape
    _, uppers, _, count, _ = near.shape
    for core, (near_blocks, far_blocks) in enumerate(((near, far), (near_core, far_core))):
        for j in range(3):
            block = lambda u, i: near_blocks[j, u, i]
            join(2 * j + core, lower, position[0], uppers, count, range(branches), block, highs, lows)
        block = lambda u, i: far_blocks[u, i * count : (i + 1) * count, :]
        join(6 + core, lower, position[0], uppers, count, range(branches), block, highs, lows)
    parts, _, taps, lanes = table.shape
    for n in range(branches):
        row = branches * count + n * taps
        for p in range(parts):
            table[p, n] = far[0, row : row + taps, p * lanes : (p + 1) * lanes]


def next_part(position, near, near_core, far, far_core, like, lower):
    table, highs, lows = (jax.ShapeDtypeStruct(w.shape, w.dtype) for w in like)
    work = pl.CostEstimate(flops=0, bytes_accessed=16 * near.size, transcendentals=0)
    operands = (position, near, near_core, far, far_core)
    kernel = functools.partial(next_kernel, lower)
    highs, lows, table = call(kernel, (highs, lows, table), operands, [], 1, work)
    return table, highs, lows


def first_kernel(n_far, n_taps, lower, position, newest, pair, highs_in, lows_in, *refs):
    far, taps, refs = refs[:n_far], refs[n_far : n_far + n_taps], refs[n_far + n_taps :]
    out, highs, lows, table, earlier, first, second, sem = refs
    load = begin(pair.at[0], earlier, sem.at[0])
    branches, channels, _ = highs.shape
    half = branches // 2
    if n_taps == 1:
        table[...] = taps[0][...]
    else:
        chip = position[0] // 2
        below = far[2]
        for j, part in enumerate(taps):
            row = below.shape[1] - (n_taps - j) * TAP_ROWS
            for n in range(branches):
                table[chip ^ j, n] = part[n]
                lanes = slice(n * LANES, (n + 1) * LANES)
                table[chip ^ (j + 2), n] = below[0, row : row + 9, lanes]
    join_far(far, lower, position[0], highs, lows)
    first[...] = separable(newest, table, highs, lows, 0)
    load.wait()
    first[...] += separable(earlier, table, highs, lows, 1)
    second[...] = separable(first, table, highs, lows, 2) + newest[...]
    out[...] = separable(second, table, highs, lows, 3) + first[...]


def first_part(position, newest, pair, matrices, far, lower, taps):
    shape, channels = newest.shape, newest.shape[-1]
    branches = matrices[0].shape[0]
    lanes = min(LANES, channels)
    like = [jax.ShapeDtypeStruct(m.shape, m.dtype) for m in matrices]
    return call(
        functools.partial(first_kernel, len(far), len(taps), lower),
        (
            jax.ShapeDtypeStruct(shape, F32),
            *like,
            jax.ShapeDtypeStruct((channels // lanes, branches, 9, lanes), F32),
        ),
        (position, newest, pair, *matrices, *far, *taps),
        [(shape, F32)] * 3,
        1,
        cost(shape, 4),
        apart=(2,),
        aliases={3: 1, 4: 2},
    )


def doubled(x, axis, bit, dim):
    other = swap(x, axis, bit)
    upper = (lax.axis_index(axis) & bit) != 0
    return jnp.where(upper, jnp.concatenate([other, x], dim), jnp.concatenate([x, other], dim))


def near_taps(taps, axis):
    size = lax.axis_size(axis)
    branches, count, width = taps.shape
    if size == 8 and 2 * width == LANES:
        chip = doubled(taps, axis, 1, 2)
        return chip, swap(chip, axis, 2)
    if size & (size - 1):
        taps = lax.all_gather(taps, axis, axis=2, tiled=True)
    else:
        bit = 1
        while bit < size:
            taps = doubled(taps, axis, bit, 2)
            bit *= 2
    channels = taps.shape[-1]
    lanes = min(LANES, channels)
    taps = taps.reshape(branches, count, channels // lanes, lanes)
    return (taps.transpose(2, 0, 1, 3),)


def from_neighbours(shard, axis):
    shard = shard[None]
    bit = 8
    while bit < lax.axis_size(axis):
        shard = doubled(shard, axis, bit, 0)
        bit *= 2
    return shard, swap(shard, axis, 2), swap(shard, axis, 4)


def body(pair, stems, taps, matrices):
    section = lax.axis_index("section").astype(jnp.int32).reshape(1)
    position = lax.axis_index("dp").astype(jnp.int32).reshape(1)
    stems = stems[:, 0]
    ticks = stems.shape[0] + 1
    pair = pair[0, :, 0]
    shard = matrices[0]
    newest = pair[1]
    size = lax.axis_size("dp")
    simple = size & (size - 1) or size < 8
    lower = 1 if simple else 8
    taps = near_taps(after(taps[0], section, position), "dp")
    passed_on = from_behind(after(newest, taps[0]), "section", around=True)
    far = ()
    if simple:
        partial = near_part(position, {0: lax.all_gather(shard, "dp")}, lower)
    else:
        own, x, y = from_neighbours(shard, "dp")
        near = {0: own, 1: swap(own, "dp", 1), 2: x, 4: y}
        two = half_of(after(x, near[1]), 1, *(taps if len(taps) > 1 else ()))
        one = half_of(y, 0)
        x_late, y_late = after(x, two), after(y, one)
        near.update({3: swap(x_late, "dp", 1), 5: swap(y_late, "dp", 1)})
        one, two = swap(one, "dp", 2), swap(two, "dp", 4)
        partial = near_part(after(position, passed_on), near, lower)
        one, two, *_ = lax.optimization_barrier((one, two, *partial))
        far = (one, swap(one, "dp", 1), two, swap(two, "dp", 1))
    output, *weights, table = first_part(position, newest, pair, partial, far, lower, taps)
    weights = (table, *weights)

    if simple:
        next_shard = lax.all_gather(from_ahead(shard, "section"), "dp")
        next_weights = (from_ahead(table, "section"), *near_part(position, {0: next_shard}, lower))
    else:
        near = lax.optimization_barrier((own, x, y, *partial))[:3]
        next_near = from_ahead(stack(*near), "section")
        rows = far[0].shape[1]
    emitted = None
    held = (1, 0, newest)
    for tick in range(1, ticks - 1):
        earlier, newest, past = passed_on, from_behind(output, "section"), output
        if tick > 1:
            earlier = after(earlier, output)
        passed_on = from_behind(newest, "section", 1)
        early = early_part(tick, min(tick, 2), section, stems, earlier, weights)
        if tick == 1 and not simple:
            next_far = from_ahead(pack(after(far[0], early), far[2], table, rows), "section")
        emitted, output = late_part(
            tick, 1, section, stems, newest, early, weights, past, emitted, 12 if tick > 1 else 2
        )
        held = (tick, 1, newest)
        last_early = early

    if not simple:
        next_near, next_far, _ = lax.optimization_barrier((next_near, next_far, last_early))
        blocks = next_near, swap(next_near, "dp", 1), next_far, swap(next_far, "dp", 1)
        next_weights = next_part(position, *blocks, weights, lower)
    early = early_part(held[0], held[1], section, stems, held[2], next_weights)
    emitted, ahead = late_part(
        ticks - 1, 0, section, stems, output, early, next_weights, output, emitted
    )
    got = from_behind(ahead, "section")
    emitted = last_part(section, got, stem_part(stems, weights), emitted)
    return emitted[None, :, None]


def solution(mesh):
    placed = (
        P("section", None, "dp", None, None, None),
        P(None, "dp", None, None, None),
        P("section", None, None, "dp"),
        P("section", None, "dp", None),
    )
    return jax.shard_map(
        body,
        mesh=mesh,
        in_specs=placed,
        out_specs=P("section", None, "dp", None, None, None),
        check_vma=False,
    )
```

```python
import functools

import jax
import jax.numpy as jnp
from jax import lax
from jax.experimental import pallas as pl
from jax.experimental.pallas import tpu as pltpu
from jax.sharding import PartitionSpec as P

F32 = jnp.float32
BF16 = jnp.bfloat16
VMEM_LIMIT = 16 * 1024 * 1024
LANES = 128
DEPTH = 256
TAP_ROWS = 16


def swap(x, axis, bit):
    size = lax.axis_size(axis)
    return lax.ppermute(x, axis, [(i, i ^ bit) for i in range(size)])


def from_behind(x, axis, first=0, around=False):
    size = lax.axis_size(axis)
    pairs = [(i, i + 1) for i in range(first, size - 1)]
    return lax.ppermute(x, axis, pairs + [(size - 1, 0)] * (around and size > 1))


def from_ahead(x, axis):
    return lax.ppermute(x, axis, [(i + 1, i) for i in range(lax.axis_size(axis) - 1)])


def after(x, *others):
    return lax.optimization_barrier((x, *others))[0]


def begin(source, target, sem):
    copy = pltpu.make_async_copy(source, target, sem)
    copy.start()
    return copy


def split(x):
    high = x.astype(BF16)
    return high, (x - high.astype(F32)).astype(BF16)


def call(kernel, outs, operands, scratch, copies, cost, apart=(), outs_apart=(), aliases=None, limit=VMEM_LIMIT):
    def spec(x, i, apart):
        space = pl.ANY if i in apart else pltpu.SMEM if x.dtype == jnp.int32 else pltpu.VMEM
        return pl.BlockSpec(memory_space=space)

    return pl.pallas_call(
        kernel,
        out_shape=outs,
        in_specs=[spec(x, i, apart) for i, x in enumerate(operands)],
        out_specs=tuple(spec(x, i, outs_apart) for i, x in enumerate(outs)),
        scratch_shapes=[pltpu.VMEM(*s) for s in scratch] + [pltpu.SemaphoreType.DMA((copies,))],
        input_output_aliases=aliases or {},
        compiler_params=pltpu.CompilerParams(vmem_limit_bytes=limit),
        cost_estimate=cost,
    )(*operands)


def cost(shape, convolutions):
    rows, columns, channels = shape
    size = rows * columns * channels
    return pl.CostEstimate(
        flops=6 * convolutions * size * channels,
        bytes_accessed=4 * (3 * size + convolutions * channels * channels),
        transcendentals=0,
    )


def shifted(u, by):
    side = u.shape[1]
    column = lax.broadcasted_iota(jnp.int32, u.shape, 1)
    outside = 0 if by == 1 else side - 1
    return jnp.where(column == outside, 0.0, pltpu.roll(u, by % side, 1))


def depthwise(source, table, branch, part, width):
    low = part * width
    if not isinstance(part, int):
        low = pl.multiple_of(low, width)
    x = jnp.maximum(source[:, :, pl.ds(low, width)], 0.0)
    nothing = jnp.zeros((1,) + x.shape[1:], F32)
    above = jnp.concatenate([nothing, x[:-1]], 0)
    below = jnp.concatenate([x[1:], nothing], 0)
    tap = [table[part, branch, k : k + 1, :].reshape(1, 1, width) for k in range(9)]
    by_column = [above * tap[j] + x * tap[3 + j] + below * tap[6 + j] for j in range(3)]
    return shifted(by_column[0], 1) + by_column[1] + shifted(by_column[2], -1)


def separable(source, table, highs, lows, branch, blocks=None):
    rows, columns, channels = source.shape
    width = min(LANES, channels)
    depth = min(DEPTH, channels)
    each = depth // width
    total = None
    for block in range(channels // depth) if blocks is None else blocks:
        mixed_in = []
        for i in range(each):
            value = depthwise(source, table, branch, block * each + i, width)
            mixed_in.append(split(value.reshape(rows * columns, width)))
        high = jnp.concatenate([p[0] for p in mixed_in], 1)
        low = jnp.concatenate([p[1] for p in mixed_in], 1)
        k = block * depth
        if not isinstance(block, int):
            k = pl.multiple_of(k, depth)
        matrix_high = highs[branch, pl.ds(k, depth), :]
        matrix_low = lows[branch, pl.ds(k, depth), :]
        both = jnp.concatenate([high, low], 0)
        product = jnp.dot(both, matrix_high, preferred_element_type=F32)
        product = product[: high.shape[0]] + product[high.shape[0] :]
        product = product + jnp.dot(high, matrix_low, preferred_element_type=F32)
        total = product if total is None else total + product
    return total.reshape(source.shape)


def fetch(tick, at, section, stems, got, held, sem):
    for s in range(at):

        @pl.when(section == s)
        def _(s=s):
            begin(stems.at[tick - 1 - s], held, sem)

    @pl.when(section >= at)
    def _():
        begin(got, held, sem)

    return pltpu.make_async_copy(got, held, sem)


def early_kernel(tick, at, section, stems, got, table, highs, lows, out, held, sem):
    fetch(tick, at, section[0], stems, got, held, sem.at[0]).wait()
    out[...] = separable(held, table, highs, lows, 1)


def late_kernel(tick, at, section, stems, got, early, table, highs, lows, past, *rest):
    emitted, out, newest, first, second, sem = rest[-6:]
    store = begin(past, emitted.at[tick - 1], sem.at[1])
    fetch(tick, at, section[0], stems, got, newest, sem.at[0]).wait()
    first[...] = separable(newest, table, highs, lows, 0) + early[...]
    second[...] = separable(first, table, highs, lows, 2) + newest[...]
    out[...] = separable(second, table, highs, lows, 3) + first[...]
    store.wait()


def early_part(tick, at, section, stems, got, weights):
    shape = got.shape
    return call(
        functools.partial(early_kernel, tick, at),
        (jax.ShapeDtypeStruct(shape, F32),),
        (section, stems, got, *weights),
        [(shape, F32)],
        1,
        cost(shape, 1),
        apart=(1, 2),
    )[0]


def late_part(tick, at, section, stems, got, early, weights, past, emitted, weight=2):
    shape = got.shape
    whole = jax.ShapeDtypeStruct((stems.shape[0] + 1,) + shape, F32)
    operands = (section, stems, got, early, *weights, past)
    return call(
        functools.partial(late_kernel, tick, at),
        (whole, jax.ShapeDtypeStruct(shape, F32)),
        operands if emitted is None else operands + (emitted,),
        [(shape, F32)] * 3,
        2,
        cost(shape, 3 * weight),
        apart=(1, 2, 8),
        outs_apart=(0,),
        aliases=None if emitted is None else {8: 0},
    )


def stem_kernel(stems, table, highs, lows, out, held, first, second, sem):
    begin(stems.at[stems.shape[0] - 1], held, sem.at[0]).wait()
    first[...] = separable(held, table, highs, lows, 0)
    first[...] += separable(held, table, highs, lows, 1)
    second[...] = separable(first, table, highs, lows, 2) + held[...]
    out[...] = separable(second, table, highs, lows, 3) + first[...]


def stem_part(stems, weights):
    shape = stems.shape[1:]
    a_map = jax.ShapeDtypeStruct(shape, F32)
    scratch = [(shape, F32)] * 3
    operands = (stems, *weights)
    return call(stem_kernel, (a_map,), operands, scratch, 1, cost(shape, 4), apart=(0,))[0]


def last_kernel(section, got, own, _, emitted, sem):
    target = emitted.at[emitted.shape[0] - 1]

    @pl.when(section[0] == 0)
    def _():
        begin(own, target, sem.at[0])

    @pl.when(section[0] > 0)
    def _():
        begin(got, target, sem.at[0])

    pltpu.make_async_copy(got, target, sem.at[0]).wait()


def last_part(section, got, own, emitted):
    whole = jax.ShapeDtypeStruct(emitted.shape, F32)
    work = pl.CostEstimate(flops=0, bytes_accessed=8 * got.size, transcendentals=0)
    operands = (section, got, own, emitted)
    return call(
        last_kernel, (whole,), operands, [], 1, work, apart=(3,), outs_apart=(0,), aliases={3: 0}
    )[0]


def join(key, lower, position, uppers, count, branches, block, highs, lows):
    for u in range(uppers):
        at = u * lower + ((position & (lower - 1)) ^ key)
        row = pl.multiple_of(at * count, count)
        for i in branches:
            high, low = split(block(u, i))
            highs[i, pl.ds(row, count), :] = high
            lows[i, pl.ds(row, count), :] = low


def near_kernel(keys, lower, position, *refs):
    pieces, (highs, lows, _) = refs[:-3], refs[-3:]
    for key, piece in zip(keys, pieces):
        uppers, branches, count, _ = piece.shape
        block = lambda u, i, piece=piece: piece[u, i]
        join(key, lower, position[0], uppers, count, range(branches), block, highs, lows)


def near_part(position, blocks, lower):
    uppers, branches, _, channels = blocks[0].shape
    matrices = jax.ShapeDtypeStruct((branches, channels, channels), BF16)
    return call(
        functools.partial(near_kernel, list(blocks), lower),
        (matrices, matrices),
        (position, *blocks.values()),
        [],
        1,
        pl.CostEstimate(flops=0, bytes_accessed=8 * matrices.size, transcendentals=0),
    )


def half_kernel(start, block, *refs):
    taps, (out, sem) = refs[:-2], refs[-2:]
    uppers, branches, count, _ = block.shape
    half = branches // 2
    copies = []
    for u in range(uppers):
        for i in range(half):
            target = out.at[u, pl.ds(i * count, count)]
            copies.append(begin(block.at[u, start + i], target, sem.at[u * half + i]))
    for j, chip in enumerate(taps):
        row = half * count + j * TAP_ROWS
        for n in range(branches):
            out[0, row : row + 9, n * LANES : (n + 1) * LANES] = chip[n]
    for copy in copies:
        copy.wait()


def half_of(block, start, *taps):
    uppers, branches, count, channels = block.shape
    half = branches // 2
    out = jax.ShapeDtypeStruct((uppers, half * count + TAP_ROWS * len(taps), channels), F32)
    work = pl.CostEstimate(flops=0, bytes_accessed=4 * block.size, transcendentals=0)
    kernel = functools.partial(half_kernel, start * half)
    return call(kernel, (out,), (block, *taps), [], half * uppers, work)[0]


def join_far(far, lower, position, highs, lows):
    branches, channels, _ = highs.shape
    half = branches // 2
    for j, piece in enumerate(far):
        uppers = piece.shape[0]
        count = channels // (uppers * lower)
        which = range(half) if j < 2 else range(half, branches)

        def block(u, i, piece=piece, which=which, count=count):
            at = (i - which[0]) * count
            return piece[u, at : at + count, :]

        join(6 + j % 2, lower, position, uppers, count, which, block, highs, lows)


def stack_kernel(*refs):
    pieces, (out, sem) = refs[:-2], refs[-2:]
    copies = [begin(piece, out.at[i], sem.at[i]) for i, piece in enumerate(pieces)]
    for copy in copies:
        copy.wait()


def stack(*pieces):
    n = len(pieces)
    out = jax.ShapeDtypeStruct((n,) + pieces[0].shape, F32)
    work = pl.CostEstimate(flops=0, bytes_accessed=8 * n * pieces[0].size, transcendentals=0)
    return call(stack_kernel, (out,), pieces, [], n, work, apart=range(n))[0]


def table_rows(table):
    return -(-table.shape[1] * table.shape[2] // 8) * 8


def pack_kernel(one, two, table, out, sem):
    parts, branches, count, lanes = table.shape
    rows = (out.shape[1] - table_rows(table)) // 2
    copies = []
    for i, piece in enumerate((one, two)):
        source = piece.at[:, pl.ds(0, rows)]
        copies.append(begin(source, out.at[:, pl.ds(i * rows, rows)], sem.at[i]))
    for n in range(branches):
        row = 2 * rows + n * count
        for p in range(parts):
            out[0, row : row + count, p * lanes : (p + 1) * lanes] = table[p, n]
    for copy in copies:
        copy.wait()


def pack(one, two, table, rows):
    uppers, _, channels = one.shape
    out = jax.ShapeDtypeStruct((uppers, 2 * rows + table_rows(table), channels), F32)
    work = pl.CostEstimate(flops=0, bytes_accessed=16 * one.size, transcendentals=0)
    return call(pack_kernel, (out,), (one, two, table), [], 2, work)[0]


def next_kernel(lower, position, near, near_core, far, far_core, highs, lows, table, _):
    branches, channels, _ = highs.shape
    _, uppers, _, count, _ = near.shape
    for core, (near_blocks, far_blocks) in enumerate(((near, far), (near_core, far_core))):
        for j in range(3):
            block = lambda u, i: near_blocks[j, u, i]
            join(2 * j + core, lower, position[0], uppers, count, range(branches), block, highs, lows)
        block = lambda u, i: far_blocks[u, i * count : (i + 1) * count, :]
        join(6 + core, lower, position[0], uppers, count, range(branches), block, highs, lows)
    parts, _, taps, lanes = table.shape
    for n in range(branches):
        row = branches * count + n * taps
        for p in range(parts):
            table[p, n] = far[0, row : row + taps, p * lanes : (p + 1) * lanes]


def next_part(position, near, near_core, far, far_core, like, lower):
    table, highs, lows = (jax.ShapeDtypeStruct(w.shape, w.dtype) for w in like)
    work = pl.CostEstimate(flops=0, bytes_accessed=16 * near.size, transcendentals=0)
    operands = (position, near, near_core, far, far_core)
    kernel = functools.partial(next_kernel, lower)
    highs, lows, table = call(kernel, (highs, lows, table), operands, [], 1, work)
    return table, highs, lows


def ahead_kernel(position, newest, pair, highs, lows, *refs):
    taps, (out, table, earlier, sem) = refs[:2], refs[2:]
    load = begin(pair.at[0], earlier, sem.at[0])
    chip = position[0] // 2
    for j, part in enumerate(taps):
        for n in range(part.shape[0]):
            table[chip ^ j, n] = part[n]
    blocks = [chip // 2]
    total = separable(newest, table, highs, lows, 0, blocks)
    load.wait()
    out[...] = total + separable(earlier, table, highs, lows, 1, blocks)


def ahead_part(position, newest, pair, matrices, taps):
    shape, channels = newest.shape, newest.shape[-1]
    table = (channels // LANES,) + taps[0].shape
    return call(
        ahead_kernel,
        (jax.ShapeDtypeStruct(shape, F32),),
        (position, newest, pair, *matrices, *taps),
        [(table, F32), (shape, F32)],
        1,
        cost(shape, 1),
        apart=(2,),
    )[0]


def first_kernel(n_far, n_taps, n_sums, lower, position, newest, pair, highs_in, lows_in, *refs):
    far, taps, refs = refs[:n_far], refs[n_far : n_far + n_taps], refs[n_far + n_taps :]
    sums, (out, highs, lows, table, earlier, first, second, sem) = refs[:n_sums], refs[n_sums:]
    load = begin(pair.at[0], earlier, sem.at[0])
    branches, channels, _ = highs.shape
    chip = position[0] // 2
    if n_taps == 1:
        table[...] = taps[0][...]
    else:
        below = far[2]
        for j, part in enumerate(taps):
            row = below.shape[1] - (n_taps - j) * TAP_ROWS
            for n in range(branches):
                table[chip ^ j, n] = part[n]
                lanes = slice(n * LANES, (n + 1) * LANES)
                table[chip ^ (j + 2), n] = below[0, row : row + 9, lanes]
    join_far(far, lower, position[0], highs, lows)
    blocks = [1 - chip // 2] if sums else None
    total = separable(newest, table, highs, lows, 0, blocks)
    for part in sums:
        total = total + part[...]
    first[...] = total
    load.wait()
    first[...] += separable(earlier, table, highs, lows, 1, blocks)
    second[...] = separable(first, table, highs, lows, 2) + newest[...]
    out[...] = separable(second, table, highs, lows, 3) + first[...]


def first_part(position, newest, pair, matrices, far, lower, taps, sums):
    shape, channels = newest.shape, newest.shape[-1]
    branches = matrices[0].shape[0]
    lanes = min(LANES, channels)
    like = [jax.ShapeDtypeStruct(m.shape, m.dtype) for m in matrices]
    return call(
        functools.partial(first_kernel, len(far), len(taps), len(sums), lower),
        (
            jax.ShapeDtypeStruct(shape, F32),
            *like,
            jax.ShapeDtypeStruct((channels // lanes, branches, 9, lanes), F32),
        ),
        (position, newest, pair, *matrices, *far, *taps, *sums),
        [(shape, F32)] * 3,
        1,
        cost(shape, 4),
        apart=(2,),
        aliases={3: 1, 4: 2},
    )


def doubled(x, axis, bit, dim):
    other = swap(x, axis, bit)
    upper = (lax.axis_index(axis) & bit) != 0
    return jnp.where(upper, jnp.concatenate([other, x], dim), jnp.concatenate([x, other], dim))


def near_taps(taps, axis):
    size = lax.axis_size(axis)
    branches, count, width = taps.shape
    if size == 8 and 2 * width == LANES:
        return doubled(taps, axis, 1, 2)
    if size & (size - 1):
        taps = lax.all_gather(taps, axis, axis=2, tiled=True)
    else:
        bit = 1
        while bit < size:
            taps = doubled(taps, axis, bit, 2)
            bit *= 2
    channels = taps.shape[-1]
    lanes = min(LANES, channels)
    taps = taps.reshape(branches, count, channels // lanes, lanes)
    return taps.transpose(2, 0, 1, 3)


def from_neighbours(shard, axis):
    shard = shard[None]
    bit = 8
    while bit < lax.axis_size(axis):
        shard = doubled(shard, axis, bit, 0)
        bit *= 2
    return shard, swap(shard, axis, 2), swap(shard, axis, 4)


def body(pair, stems, taps, matrices):
    section = lax.axis_index("section").astype(jnp.int32).reshape(1)
    position = lax.axis_index("dp").astype(jnp.int32).reshape(1)
    stems = stems[:, 0]
    ticks = stems.shape[0] + 1
    pair = pair[0, :, 0]
    shard = matrices[0]
    newest = pair[1]
    size = lax.axis_size("dp")
    simple = size & (size - 1) or size < 8
    lower = 1 if simple else 8
    taps = near_taps(after(taps[0], section, position), "dp")
    newest, taps = lax.optimization_barrier((newest, taps))
    taps = (taps, swap(taps, "dp", 2)) if taps.ndim == 3 else (taps,)
    passed_on = from_behind(newest, "section", around=True)
    far = sums = ()
    channels = newest.shape[-1]
    if simple:
        partial = near_part(position, {0: lax.all_gather(shard, "dp")}, lower)
    else:
        own, x, y = from_neighbours(shard, "dp")
        near = {0: own, 1: swap(own, "dp", 1), 2: x, 4: y}
        two = half_of(after(x, near[1]), 1, *(taps if len(taps) > 1 else ()))
        one = half_of(y, 0)
        x_late, y_late = after(x, two), after(y, one)
        near.update({3: swap(x_late, "dp", 1), 5: swap(y_late, "dp", 1)})
        one, two = swap(one, "dp", 2), swap(two, "dp", 4)
        partial = near_part(position, near, lower)
        if len(taps) > 1 and channels == 2 * DEPTH:
            sums = (ahead_part(after(position, passed_on), newest, pair, partial, taps),)
        one, two, *_ = lax.optimization_barrier((one, two, passed_on, *partial, *sums))
        far = (one, swap(one, "dp", 1), two, swap(two, "dp", 1))
    output, *weights, table = first_part(
        position, newest, pair, partial, far, lower, taps, sums
    )
    weights = (table, *weights)

    if simple:
        next_shard = lax.all_gather(from_ahead(shard, "section"), "dp")
        next_weights = (from_ahead(table, "section"), *near_part(position, {0: next_shard}, lower))
    else:
        near = lax.optimization_barrier((own, x, y, *partial))[:3]
        next_near = from_ahead(stack(*near), "section")
        rows = far[0].shape[1]
    emitted = None
    held = (1, 0, newest)
    for tick in range(1, ticks - 1):
        earlier, newest, past = passed_on, from_behind(output, "section"), output
        if tick > 1:
            earlier = after(earlier, output)
        passed_on = from_behind(newest, "section", 1)
        early = early_part(tick, min(tick, 2), section, stems, earlier, weights)
        if tick == 1 and not simple:
            next_far = from_ahead(pack(after(far[0], early), far[2], table, rows), "section")
        emitted, output = late_part(
            tick, 1, section, stems, newest, early, weights, past, emitted, 12 if tick > 1 else 2
        )
        held = (tick, 1, newest)
        last_early = early

    if not simple:
        next_near, next_far, _ = lax.optimization_barrier((next_near, next_far, last_early))
        blocks = next_near, swap(next_near, "dp", 1), next_far, swap(next_far, "dp", 1)
        next_weights = next_part(position, *blocks, weights, lower)
    early = early_part(held[0], held[1], section, stems, held[2], next_weights)
    emitted, ahead = late_part(
        ticks - 1, 0, section, stems, output, early, next_weights, output, emitted
    )
    got = from_behind(ahead, "section")
    emitted = last_part(section, got, stem_part(stems, weights), emitted)
    return emitted[None, :, None]


def solution(mesh):
    placed = (
        P("section", None, "dp", None, None, None),
        P(None, "dp", None, None, None),
        P("section", None, None, "dp"),
        P("section", None, "dp", None),
    )
    return jax.shard_map(
        body,
        mesh=mesh,
        in_specs=placed,
        out_specs=P("section", None, "dp", None, None, None),
        check_vma=False,
    )
```

```python
import functools

import jax
import jax.numpy as jnp
from jax import lax
from jax.experimental import pallas as pl
from jax.experimental.pallas import tpu as pltpu
from jax.sharding import PartitionSpec as P

F32 = jnp.float32
BF16 = jnp.bfloat16
VMEM_LIMIT = 16 * 1024 * 1024
LANES = 128
DEPTH = 256


def swap(x, axis, bit):
    size = lax.axis_size(axis)
    return lax.ppermute(x, axis, [(i, i ^ bit) for i in range(size)])


def from_behind(x, axis, first=0, around=False):
    size = lax.axis_size(axis)
    pairs = [(i, i + 1) for i in range(first, size - 1)]
    return lax.ppermute(x, axis, pairs + [(size - 1, 0)] * (around and size > 1))


def from_ahead(x, axis):
    return lax.ppermute(x, axis, [(i + 1, i) for i in range(lax.axis_size(axis) - 1)])


def after(x, *others):
    return lax.optimization_barrier((x, *others))[0]


def begin(source, target, sem):
    copy = pltpu.make_async_copy(source, target, sem)
    copy.start()
    return copy


def split(x):
    high = x.astype(BF16)
    return high, (x - high.astype(F32)).astype(BF16)


def call(kernel, outs, operands, scratch, copies, cost, apart=(), outs_apart=(), aliases=None, limit=VMEM_LIMIT):
    def spec(x, i, apart):
        space = pl.ANY if i in apart else pltpu.SMEM if x.dtype == jnp.int32 else pltpu.VMEM
        return pl.BlockSpec(memory_space=space)

    return pl.pallas_call(
        kernel,
        out_shape=outs,
        in_specs=[spec(x, i, apart) for i, x in enumerate(operands)],
        out_specs=tuple(spec(x, i, outs_apart) for i, x in enumerate(outs)),
        scratch_shapes=[pltpu.VMEM(*s) for s in scratch] + [pltpu.SemaphoreType.DMA((copies,))],
        input_output_aliases=aliases or {},
        compiler_params=pltpu.CompilerParams(vmem_limit_bytes=limit),
        cost_estimate=cost,
    )(*operands)


def cost(shape, convolutions):
    rows, columns, channels = shape
    size = rows * columns * channels
    return pl.CostEstimate(
        flops=6 * convolutions * size * channels,
        bytes_accessed=4 * (3 * size + convolutions * channels * channels),
        transcendentals=0,
    )


def shifted(u, by):
    side = u.shape[1]
    column = lax.broadcasted_iota(jnp.int32, u.shape, 1)
    outside = 0 if by == 1 else side - 1
    return jnp.where(column == outside, 0.0, pltpu.roll(u, by % side, 1))


def depthwise(source, table, branch, part, width):
    low = part * width
    if not isinstance(part, int):
        low = pl.multiple_of(low, width)
    x = jnp.maximum(source[:, :, pl.ds(low, width)], 0.0)
    nothing = jnp.zeros((1,) + x.shape[1:], F32)
    above = jnp.concatenate([nothing, x[:-1]], 0)
    below = jnp.concatenate([x[1:], nothing], 0)
    tap = [table[part, branch, k : k + 1, :].reshape(1, 1, width) for k in range(9)]
    by_column = [above * tap[j] + x * tap[3 + j] + below * tap[6 + j] for j in range(3)]
    return shifted(by_column[0], 1) + by_column[1] + shifted(by_column[2], -1)


def separable(source, table, highs, lows, branch, blocks=None):
    rows, columns, channels = source.shape
    width = min(LANES, channels)
    depth = min(DEPTH, channels)
    each = depth // width
    total = None
    for block in range(channels // depth) if blocks is None else blocks:
        mixed_in = []
        for i in range(each):
            value = depthwise(source, table, branch, block * each + i, width)
            mixed_in.append(split(value.reshape(rows * columns, width)))
        high = jnp.concatenate([p[0] for p in mixed_in], 1)
        low = jnp.concatenate([p[1] for p in mixed_in], 1)
        k = block * depth
        if not isinstance(block, int):
            k = pl.multiple_of(k, depth)
        matrix_high = highs[branch, pl.ds(k, depth), :]
        matrix_low = lows[branch, pl.ds(k, depth), :]
        both = jnp.concatenate([high, low], 0)
        product = jnp.dot(both, matrix_high, preferred_element_type=F32)
        product = product[: high.shape[0]] + product[high.shape[0] :]
        product = product + jnp.dot(high, matrix_low, preferred_element_type=F32)
        total = product if total is None else total + product
    return total.reshape(source.shape)


def fetch(tick, at, section, stems, got, held, sem):
    for s in range(at):

        @pl.when(section == s)
        def _(s=s):
            begin(stems.at[tick - 1 - s], held, sem)

    @pl.when(section >= at)
    def _():
        begin(got, held, sem)

    return pltpu.make_async_copy(got, held, sem)


def early_kernel(tick, at, section, stems, got, table, highs, lows, out, held, sem):
    fetch(tick, at, section[0], stems, got, held, sem.at[0]).wait()
    out[...] = separable(held, table, highs, lows, 1)


def late_kernel(tick, at, section, stems, got, early, table, highs, lows, past, *rest):
    emitted, out, newest, first, second, sem = rest[-6:]
    store = begin(past, emitted.at[tick - 1], sem.at[1])
    fetch(tick, at, section[0], stems, got, newest, sem.at[0]).wait()
    first[...] = separable(newest, table, highs, lows, 0) + early[...]
    second[...] = separable(first, table, highs, lows, 2) + newest[...]
    out[...] = separable(second, table, highs, lows, 3) + first[...]
    store.wait()


def early_part(tick, at, section, stems, got, weights):
    shape = got.shape
    return call(
        functools.partial(early_kernel, tick, at),
        (jax.ShapeDtypeStruct(shape, F32),),
        (section, stems, got, *weights),
        [(shape, F32)],
        1,
        cost(shape, 1),
        apart=(1, 2),
    )[0]


def late_part(tick, at, section, stems, got, early, weights, past, emitted, weight=2):
    shape = got.shape
    whole = jax.ShapeDtypeStruct((stems.shape[0] + 1,) + shape, F32)
    operands = (section, stems, got, early, *weights, past)
    return call(
        functools.partial(late_kernel, tick, at),
        (whole, jax.ShapeDtypeStruct(shape, F32)),
        operands if emitted is None else operands + (emitted,),
        [(shape, F32)] * 3,
        2,
        cost(shape, 3 * weight),
        apart=(1, 2, 8),
        outs_apart=(0,),
        aliases=None if emitted is None else {8: 0},
    )


def stem_kernel(stems, table, highs, lows, out, held, first, second, sem):
    begin(stems.at[stems.shape[0] - 1], held, sem.at[0]).wait()
    first[...] = separable(held, table, highs, lows, 0)
    first[...] += separable(held, table, highs, lows, 1)
    second[...] = separable(first, table, highs, lows, 2) + held[...]
    out[...] = separable(second, table, highs, lows, 3) + first[...]


def stem_part(stems, weights):
    shape = stems.shape[1:]
    a_map = jax.ShapeDtypeStruct(shape, F32)
    scratch = [(shape, F32)] * 3
    operands = (stems, *weights)
    return call(stem_kernel, (a_map,), operands, scratch, 1, cost(shape, 4), apart=(0,))[0]


def last_kernel(section, got, own, _, emitted, sem):
    target = emitted.at[emitted.shape[0] - 1]

    @pl.when(section[0] == 0)
    def _():
        begin(own, target, sem.at[0])

    @pl.when(section[0] > 0)
    def _():
        begin(got, target, sem.at[0])

    pltpu.make_async_copy(got, target, sem.at[0]).wait()


def last_part(section, got, own, emitted):
    whole = jax.ShapeDtypeStruct(emitted.shape, F32)
    work = pl.CostEstimate(flops=0, bytes_accessed=8 * got.size, transcendentals=0)
    operands = (section, got, own, emitted)
    return call(
        last_kernel, (whole,), operands, [], 1, work, apart=(3,), outs_apart=(0,), aliases={3: 0}
    )[0]


def join(key, lower, position, uppers, count, branches, block, highs, lows):
    for u in range(uppers):
        at = u * lower + ((position & (lower - 1)) ^ key)
        row = pl.multiple_of(at * count, count)
        for i in branches:
            high, low = split(block(u, i))
            highs[i, pl.ds(row, count), :] = high
            lows[i, pl.ds(row, count), :] = low


def near_kernel(keys, lower, position, *refs):
    pieces, (highs, lows, _) = refs[:-3], refs[-3:]
    for key, piece in zip(keys, pieces):
        uppers, branches, count, _ = piece.shape
        block = lambda u, i, piece=piece: piece[u, i]
        join(key, lower, position[0], uppers, count, range(branches), block, highs, lows)


def near_part(position, blocks, lower):
    uppers, branches, _, channels = blocks[0].shape
    matrices = jax.ShapeDtypeStruct((branches, channels, channels), BF16)
    return call(
        functools.partial(near_kernel, list(blocks), lower),
        (matrices, matrices),
        (position, *blocks.values()),
        [],
        1,
        pl.CostEstimate(flops=0, bytes_accessed=8 * matrices.size, transcendentals=0),
    )


def half_kernel(start, block, *refs):
    taps, (out, sem) = refs[:-2], refs[-2:]
    uppers, branches, count, _ = block.shape
    half = branches // 2
    copies = []
    for u in range(uppers):
        for i in range(half):
            target = out.at[u, pl.ds(i * count, count)]
            copies.append(begin(block.at[u, start + i], target, sem.at[u * half + i]))
    for j, chip in enumerate(taps):
        row = half * count + j * chip.shape[1]
        for n in range(branches):
            out[0, row : row + 9, n * LANES : (n + 1) * LANES] = chip[n]
    for copy in copies:
        copy.wait()


def half_of(block, start, *taps):
    uppers, branches, count, channels = block.shape
    half = branches // 2
    extra = -(-sum(chip.shape[1] for chip in taps) // 8) * 8
    out = jax.ShapeDtypeStruct((uppers, half * count + extra, channels), F32)
    work = pl.CostEstimate(flops=0, bytes_accessed=4 * block.size, transcendentals=0)
    kernel = functools.partial(half_kernel, start * half)
    return call(kernel, (out,), (block, *taps), [], half * uppers, work)[0]


def join_far(far, lower, position, highs, lows):
    branches, channels, _ = highs.shape
    half = branches // 2
    for j, piece in enumerate(far):
        uppers = piece.shape[0]
        count = channels // (uppers * lower)
        which = range(half) if j < 2 else range(half, branches)

        def block(u, i, piece=piece, which=which, count=count):
            at = (i - which[0]) * count
            return piece[u, at : at + count, :]

        join(6 + j % 2, lower, position, uppers, count, which, block, highs, lows)


def stack_kernel(*refs):
    pieces, (out, sem) = refs[:-2], refs[-2:]
    copies = [begin(piece, out.at[i], sem.at[i]) for i, piece in enumerate(pieces)]
    for copy in copies:
        copy.wait()


def stack(*pieces):
    n = len(pieces)
    out = jax.ShapeDtypeStruct((n,) + pieces[0].shape, F32)
    work = pl.CostEstimate(flops=0, bytes_accessed=8 * n * pieces[0].size, transcendentals=0)
    return call(stack_kernel, (out,), pieces, [], n, work, apart=range(n))[0]


def table_rows(table):
    return -(-table.shape[1] * table.shape[2] // 8) * 8


def pack_kernel(one, two, table, out, sem):
    parts, branches, count, lanes = table.shape
    rows = (out.shape[1] - table_rows(table)) // 2
    copies = []
    for i, piece in enumerate((one, two)):
        source = piece.at[:, pl.ds(0, rows)]
        copies.append(begin(source, out.at[:, pl.ds(i * rows, rows)], sem.at[i]))
    for n in range(branches):
        row = 2 * rows + n * count
        for p in range(parts):
            out[0, row : row + count, p * lanes : (p + 1) * lanes] = table[p, n]
    for copy in copies:
        copy.wait()


def pack(one, two, table, rows):
    uppers, _, channels = one.shape
    out = jax.ShapeDtypeStruct((uppers, 2 * rows + table_rows(table), channels), F32)
    work = pl.CostEstimate(flops=0, bytes_accessed=16 * one.size, transcendentals=0)
    return call(pack_kernel, (out,), (one, two, table), [], 2, work)[0]


def next_kernel(lower, position, near, near_core, far, far_core, highs, lows, table, _):
    branches, channels, _ = highs.shape
    _, uppers, _, count, _ = near.shape
    for core, (near_blocks, far_blocks) in enumerate(((near, far), (near_core, far_core))):
        for j in range(3):
            block = lambda u, i: near_blocks[j, u, i]
            join(2 * j + core, lower, position[0], uppers, count, range(branches), block, highs, lows)
        block = lambda u, i: far_blocks[u, i * count : (i + 1) * count, :]
        join(6 + core, lower, position[0], uppers, count, range(branches), block, highs, lows)
    parts, _, taps, lanes = table.shape
    for n in range(branches):
        row = branches * count + n * taps
        for p in range(parts):
            table[p, n] = far[0, row : row + taps, p * lanes : (p + 1) * lanes]


def next_part(position, near, near_core, far, far_core, like, lower):
    table, highs, lows = (jax.ShapeDtypeStruct(w.shape, w.dtype) for w in like)
    work = pl.CostEstimate(flops=0, bytes_accessed=16 * near.size, transcendentals=0)
    operands = (position, near, near_core, far, far_core)
    kernel = functools.partial(next_kernel, lower)
    highs, lows, table = call(kernel, (highs, lows, table), operands, [], 1, work)
    return table, highs, lows


def ahead_kernel(position, newest, pair, highs, lows, *refs):
    taps, (out, table, earlier, sem) = refs[:2], refs[2:]
    load = begin(pair.at[0], earlier, sem.at[0])
    chip = position[0] // 2
    for j, part in enumerate(taps):
        for n in range(part.shape[0]):
            table[chip ^ j, n] = part[n]
    blocks = [chip // 2]
    total = separable(newest, table, highs, lows, 0, blocks)
    load.wait()
    out[...] = total + separable(earlier, table, highs, lows, 1, blocks)


def ahead_part(position, newest, pair, matrices, taps):
    shape, channels = newest.shape, newest.shape[-1]
    table = (channels // LANES,) + taps[0].shape
    return call(
        ahead_kernel,
        (jax.ShapeDtypeStruct(shape, F32),),
        (position, newest, pair, *matrices, *taps),
        [(table, F32), (shape, F32)],
        1,
        cost(shape, 1),
        apart=(2,),
    )[0]


def first_kernel(n_far, n_taps, n_sums, lower, position, newest, pair, highs_in, lows_in, *refs):
    far, taps, refs = refs[:n_far], refs[n_far : n_far + n_taps], refs[n_far + n_taps :]
    sums, (out, highs, lows, table, earlier, first, second, sem) = refs[:n_sums], refs[n_sums:]
    load = begin(pair.at[0], earlier, sem.at[0])
    branches, channels, _ = highs.shape
    chip = position[0] // 2
    if n_taps == 1:
        table[...] = taps[0][...]
    else:
        below = far[2]
        for j, part in enumerate(taps):
            row = far[0].shape[1] + j * part.shape[1]
            for n in range(branches):
                table[chip ^ j, n] = part[n]
                lanes = slice(n * LANES, (n + 1) * LANES)
                table[chip ^ (j + 2), n] = below[0, row : row + 9, lanes]
    join_far(far, lower, position[0], highs, lows)
    blocks = [1 - chip // 2] if sums else None
    total = separable(newest, table, highs, lows, 0, blocks)
    for part in sums:
        total = total + part[...]
    first[...] = total
    load.wait()
    first[...] += separable(earlier, table, highs, lows, 1, blocks)
    second[...] = separable(first, table, highs, lows, 2) + newest[...]
    out[...] = separable(second, table, highs, lows, 3) + first[...]


def first_part(position, newest, pair, matrices, far, lower, taps, sums):
    shape, channels = newest.shape, newest.shape[-1]
    branches = matrices[0].shape[0]
    lanes = min(LANES, channels)
    like = [jax.ShapeDtypeStruct(m.shape, m.dtype) for m in matrices]
    return call(
        functools.partial(first_kernel, len(far), len(taps), len(sums), lower),
        (
            jax.ShapeDtypeStruct(shape, F32),
            *like,
            jax.ShapeDtypeStruct((channels // lanes, branches, 9, lanes), F32),
        ),
        (position, newest, pair, *matrices, *far, *taps, *sums),
        [(shape, F32)] * 3,
        1,
        cost(shape, 4),
        apart=(2,),
        aliases={3: 1, 4: 2},
    )


def doubled(x, axis, bit, dim):
    other = swap(x, axis, bit)
    upper = (lax.axis_index(axis) & bit) != 0
    return jnp.where(upper, jnp.concatenate([other, x], dim), jnp.concatenate([x, other], dim))


def near_taps(taps, axis):
    size = lax.axis_size(axis)
    branches, count, width = taps.shape
    if size == 8 and 2 * width == LANES:
        return doubled(taps, axis, 1, 2)
    if size & (size - 1):
        taps = lax.all_gather(taps, axis, axis=2, tiled=True)
    else:
        bit = 1
        while bit < size:
            taps = doubled(taps, axis, bit, 2)
            bit *= 2
    channels = taps.shape[-1]
    lanes = min(LANES, channels)
    taps = taps.reshape(branches, count, channels // lanes, lanes)
    return taps.transpose(2, 0, 1, 3)


def from_neighbours(shard, axis):
    shard = shard[None]
    bit = 8
    while bit < lax.axis_size(axis):
        shard = doubled(shard, axis, bit, 0)
        bit *= 2
    return shard, swap(shard, axis, 2), swap(shard, axis, 4)


def body(pair, stems, taps, matrices):
    section = lax.axis_index("section").astype(jnp.int32).reshape(1)
    position = lax.axis_index("dp").astype(jnp.int32).reshape(1)
    stems = stems[:, 0]
    ticks = stems.shape[0] + 1
    pair = pair[0, :, 0]
    shard = matrices[0]
    newest = pair[1]
    size = lax.axis_size("dp")
    simple = size & (size - 1) or size < 8
    lower = 1 if simple else 8
    taps = near_taps(after(taps[0], section, position), "dp")
    newest, taps = lax.optimization_barrier((newest, taps))
    taps = (taps, swap(taps, "dp", 2)) if taps.ndim == 3 else (taps,)
    passed_on = from_behind(newest, "section", around=True)
    far = sums = ()
    channels = newest.shape[-1]
    if simple:
        partial = near_part(position, {0: lax.all_gather(shard, "dp")}, lower)
    else:
        own, x, y = from_neighbours(shard, "dp")
        near = {0: own, 1: swap(own, "dp", 1), 2: x, 4: y}
        two = half_of(after(x, near[1]), 1, *(taps if len(taps) > 1 else ()))
        one = half_of(y, 0)
        x_late, y_late = after(x, two), after(y, one)
        near.update({3: swap(x_late, "dp", 1), 5: swap(y_late, "dp", 1)})
        one, two = swap(one, "dp", 2), swap(two, "dp", 4)
        partial = near_part(position, near, lower)
        if len(taps) > 1 and channels == 2 * DEPTH:
            sums = (ahead_part(after(position, passed_on), newest, pair, partial, taps),)
        one, two, *_ = lax.optimization_barrier((one, two, passed_on, *partial, *sums))
        far = (one, swap(one, "dp", 1), two, swap(two, "dp", 1))
    output, *weights, table = first_part(
        position, newest, pair, partial, far, lower, taps, sums
    )
    weights = (table, *weights)

    if simple:
        next_shard = lax.all_gather(from_ahead(shard, "section"), "dp")
        next_weights = (from_ahead(table, "section"), *near_part(position, {0: next_shard}, lower))
    else:
        near = lax.optimization_barrier((own, x, y, *partial))[:3]
        next_near = from_ahead(stack(*near), "section")
        rows = far[0].shape[1]
    emitted = None
    held = (1, 0, newest)
    for tick in range(1, ticks - 1):
        earlier, newest, past = passed_on, from_behind(output, "section"), output
        if tick > 1:
            earlier = after(earlier, output)
        passed_on = from_behind(newest, "section", 1)
        early = early_part(tick, min(tick, 2), section, stems, earlier, weights)
        if tick == 1 and not simple:
            next_far = from_ahead(pack(after(far[0], early), far[2], table, rows), "section")
        emitted, output = late_part(
            tick, 1, section, stems, newest, early, weights, past, emitted, 12 if tick > 1 else 2
        )
        held = (tick, 1, newest)
        last_early = early

    if not simple:
        next_near, next_far, _ = lax.optimization_barrier((next_near, next_far, last_early))
        blocks = next_near, swap(next_near, "dp", 1), next_far, swap(next_far, "dp", 1)
        next_weights = next_part(position, *blocks, weights, lower)
    early = early_part(held[0], held[1], section, stems, held[2], next_weights)
    emitted, ahead = late_part(
        ticks - 1, 0, section, stems, output, early, next_weights, output, emitted
    )
    got = from_behind(ahead, "section")
    emitted = last_part(section, got, stem_part(stems, weights), emitted)
    return emitted[None, :, None]


def solution(mesh):
    placed = (
        P("section", None, "dp", None, None, None),
        P(None, "dp", None, None, None),
        P("section", None, None, "dp"),
        P("section", None, "dp", None),
    )
    return jax.shard_map(
        body,
        mesh=mesh,
        in_specs=placed,
        out_specs=P("section", None, "dp", None, None, None),
        check_vma=False,
    )
```

```python
import functools

import jax
import jax.numpy as jnp
from jax import lax
from jax.experimental import pallas as pl
from jax.experimental.pallas import tpu as pltpu
from jax.sharding import PartitionSpec as P

F32 = jnp.float32
BF16 = jnp.bfloat16
VMEM_LIMIT = 16 * 1024 * 1024
LANES = 128
DEPTH = 256
TAP_ROWS = 16


def swap(x, axis, bit):
    size = lax.axis_size(axis)
    return lax.ppermute(x, axis, [(i, i ^ bit) for i in range(size)])


def from_behind(x, axis, first=0, around=False):
    size = lax.axis_size(axis)
    pairs = [(i, i + 1) for i in range(first, size - 1)]
    return lax.ppermute(x, axis, pairs + [(size - 1, 0)] * (around and size > 1))


def from_ahead(x, axis):
    return lax.ppermute(x, axis, [(i + 1, i) for i in range(lax.axis_size(axis) - 1)])


def after(x, *others):
    return lax.optimization_barrier((x, *others))[0]


def begin(source, target, sem):
    copy = pltpu.make_async_copy(source, target, sem)
    copy.start()
    return copy


def split(x):
    high = x.astype(BF16)
    return high, (x - high.astype(F32)).astype(BF16)


def call(kernel, outs, operands, scratch, copies, cost, apart=(), outs_apart=(), aliases=None, limit=VMEM_LIMIT):
    def spec(x, i, apart):
        space = pl.ANY if i in apart else pltpu.SMEM if x.dtype == jnp.int32 else pltpu.VMEM
        return pl.BlockSpec(memory_space=space)

    return pl.pallas_call(
        kernel,
        out_shape=outs,
        in_specs=[spec(x, i, apart) for i, x in enumerate(operands)],
        out_specs=tuple(spec(x, i, outs_apart) for i, x in enumerate(outs)),
        scratch_shapes=[pltpu.VMEM(*s) for s in scratch] + [pltpu.SemaphoreType.DMA((copies,))],
        input_output_aliases=aliases or {},
        compiler_params=pltpu.CompilerParams(vmem_limit_bytes=limit),
        cost_estimate=cost,
    )(*operands)


def cost(shape, convolutions):
    rows, columns, channels = shape
    size = rows * columns * channels
    return pl.CostEstimate(
        flops=6 * convolutions * size * channels,
        bytes_accessed=4 * (3 * size + convolutions * channels * channels),
        transcendentals=0,
    )


def shifted(u, by):
    side = u.shape[1]
    column = lax.broadcasted_iota(jnp.int32, u.shape, 1)
    outside = 0 if by == 1 else side - 1
    return jnp.where(column == outside, 0.0, pltpu.roll(u, by % side, 1))


def depthwise(source, table, branch, part, width):
    low = part * width
    if not isinstance(part, int):
        low = pl.multiple_of(low, width)
    x = jnp.maximum(source[:, :, pl.ds(low, width)], 0.0)
    nothing = jnp.zeros((1,) + x.shape[1:], F32)
    above = jnp.concatenate([nothing, x[:-1]], 0)
    below = jnp.concatenate([x[1:], nothing], 0)
    tap = [table[part, branch, k : k + 1, :].reshape(1, 1, width) for k in range(9)]
    by_column = [above * tap[j] + x * tap[3 + j] + below * tap[6 + j] for j in range(3)]
    return shifted(by_column[0], 1) + by_column[1] + shifted(by_column[2], -1)


def separable(source, table, highs, lows, branch, blocks=None):
    rows, columns, channels = source.shape
    width = min(LANES, channels)
    depth = min(DEPTH, channels)
    each = depth // width
    total = None
    for block in range(channels // depth) if blocks is None else blocks:
        mixed_in = []
        for i in range(each):
            value = depthwise(source, table, branch, block * each + i, width)
            mixed_in.append(split(value.reshape(rows * columns, width)))
        high = jnp.concatenate([p[0] for p in mixed_in], 1)
        low = jnp.concatenate([p[1] for p in mixed_in], 1)
        k = block * depth
        if not isinstance(block, int):
            k = pl.multiple_of(k, depth)
        matrix_high = highs[branch, pl.ds(k, depth), :]
        matrix_low = lows[branch, pl.ds(k, depth), :]
        both = jnp.concatenate([high, low], 0)
        product = jnp.dot(both, matrix_high, preferred_element_type=F32)
        product = product[: high.shape[0]] + product[high.shape[0] :]
        product = product + jnp.dot(high, matrix_low, preferred_element_type=F32)
        total = product if total is None else total + product
    return total.reshape(source.shape)


def fetch(tick, at, section, stems, got, held, sem):
    for s in range(at):

        @pl.when(section == s)
        def _(s=s):
            begin(stems.at[tick - 1 - s], held, sem)

    @pl.when(section >= at)
    def _():
        begin(got, held, sem)

    return pltpu.make_async_copy(got, held, sem)


def early_kernel(tick, at, section, stems, got, table, highs, lows, out, held, sem):
    fetch(tick, at, section[0], stems, got, held, sem.at[0]).wait()
    out[...] = separable(held, table, highs, lows, 1)


def late_kernel(tick, at, section, stems, got, early, table, highs, lows, past, *rest):
    emitted, out, newest, first, second, sem = rest[-6:]
    store = begin(past, emitted.at[tick - 1], sem.at[1])
    fetch(tick, at, section[0], stems, got, newest, sem.at[0]).wait()
    first[...] = separable(newest, table, highs, lows, 0) + early[...]
    second[...] = separable(first, table, highs, lows, 2) + newest[...]
    out[...] = separable(second, table, highs, lows, 3) + first[...]
    store.wait()


def early_part(tick, at, section, stems, got, weights):
    shape = got.shape
    return call(
        functools.partial(early_kernel, tick, at),
        (jax.ShapeDtypeStruct(shape, F32),),
        (section, stems, got, *weights),
        [(shape, F32)],
        1,
        cost(shape, 1),
        apart=(1, 2),
    )[0]


def late_part(tick, at, section, stems, got, early, weights, past, emitted, weight=2):
    shape = got.shape
    whole = jax.ShapeDtypeStruct((stems.shape[0] + 1,) + shape, F32)
    operands = (section, stems, got, early, *weights, past)
    return call(
        functools.partial(late_kernel, tick, at),
        (whole, jax.ShapeDtypeStruct(shape, F32)),
        operands if emitted is None else operands + (emitted,),
        [(shape, F32)] * 3,
        2,
        cost(shape, 3 * weight),
        apart=(1, 2, 8),
        outs_apart=(0,),
        aliases=None if emitted is None else {8: 0},
    )


def last_cell_kernel(tick, at, section, stems, got, newest, table, highs, lows, _, *rest):
    emitted, out, earlier, first, second, sem = rest
    load = fetch(tick, at, section[0], stems, got, earlier, sem.at[0])
    store = begin(newest, emitted.at[tick], sem.at[1])
    first[...] = separable(newest, table, highs, lows, 0)
    load.wait()
    first[...] += separable(earlier, table, highs, lows, 1)
    second[...] = separable(first, table, highs, lows, 2) + newest[...]
    out[...] = separable(second, table, highs, lows, 3) + first[...]
    store.wait()


def last_cell(tick, at, section, stems, got, newest, weights, emitted):
    shape = got.shape
    whole = jax.ShapeDtypeStruct(emitted.shape, F32)
    return call(
        functools.partial(last_cell_kernel, tick, at),
        (whole, jax.ShapeDtypeStruct(shape, F32)),
        (section, stems, got, newest, *weights, emitted),
        [(shape, F32)] * 3,
        2,
        cost(shape, 7),
        apart=(1, 2, 7),
        outs_apart=(0,),
        aliases={7: 0},
    )


def stem_kernel(stems, table, highs, lows, out, held, first, second, sem):
    begin(stems.at[stems.shape[0] - 1], held, sem.at[0]).wait()
    first[...] = separable(held, table, highs, lows, 0)
    first[...] += separable(held, table, highs, lows, 1)
    second[...] = separable(first, table, highs, lows, 2) + held[...]
    out[...] = separable(second, table, highs, lows, 3) + first[...]


def stem_part(stems, weights):
    shape = stems.shape[1:]
    a_map = jax.ShapeDtypeStruct(shape, F32)
    scratch = [(shape, F32)] * 3
    operands = (stems, *weights)
    return call(stem_kernel, (a_map,), operands, scratch, 1, cost(shape, 4), apart=(0,))[0]


def last_kernel(section, got, own, _, emitted, sem):
    target = emitted.at[emitted.shape[0] - 1]

    @pl.when(section[0] == 0)
    def _():
        begin(own, target, sem.at[0])

    @pl.when(section[0] > 0)
    def _():
        begin(got, target, sem.at[0])

    pltpu.make_async_copy(got, target, sem.at[0]).wait()


def last_part(section, got, own, emitted):
    whole = jax.ShapeDtypeStruct(emitted.shape, F32)
    work = pl.CostEstimate(flops=0, bytes_accessed=8 * got.size, transcendentals=0)
    operands = (section, got, own, emitted)
    return call(
        last_kernel, (whole,), operands, [], 1, work, apart=(3,), outs_apart=(0,), aliases={3: 0}
    )[0]


def join(key, lower, position, uppers, count, branches, block, highs, lows):
    for u in range(uppers):
        at = u * lower + ((position & (lower - 1)) ^ key)
        row = pl.multiple_of(at * count, count)
        for i in branches:
            high, low = split(block(u, i))
            highs[i, pl.ds(row, count), :] = high
            lows[i, pl.ds(row, count), :] = low


def near_kernel(keys, lower, position, *refs):
    pieces, (highs, lows, _) = refs[:-3], refs[-3:]
    for key, piece in zip(keys, pieces):
        uppers, branches, count, _ = piece.shape
        block = lambda u, i, piece=piece: piece[u, i]
        join(key, lower, position[0], uppers, count, range(branches), block, highs, lows)


def near_part(position, blocks, lower):
    uppers, branches, _, channels = blocks[0].shape
    matrices = jax.ShapeDtypeStruct((branches, channels, channels), BF16)
    return call(
        functools.partial(near_kernel, list(blocks), lower),
        (matrices, matrices),
        (position, *blocks.values()),
        [],
        1,
        pl.CostEstimate(flops=0, bytes_accessed=8 * matrices.size, transcendentals=0),
    )


def half_kernel(start, block, *refs):
    taps, (out, sem) = refs[:-2], refs[-2:]
    uppers, branches, count, _ = block.shape
    half = branches // 2
    copies = []
    for u in range(uppers):
        for i in range(half):
            target = out.at[u, pl.ds(i * count, count)]
            copies.append(begin(block.at[u, start + i], target, sem.at[u * half + i]))
    for j, chip in enumerate(taps):
        row = half * count + j * TAP_ROWS
        for n in range(branches):
            out[0, row : row + 9, n * LANES : (n + 1) * LANES] = chip[n]
    for copy in copies:
        copy.wait()


def half_of(block, start, *taps):
    uppers, branches, count, channels = block.shape
    half = branches // 2
    out = jax.ShapeDtypeStruct((uppers, half * count + TAP_ROWS * len(taps), channels), F32)
    work = pl.CostEstimate(flops=0, bytes_accessed=4 * block.size, transcendentals=0)
    kernel = functools.partial(half_kernel, start * half)
    return call(kernel, (out,), (block, *taps), [], half * uppers, work)[0]


def join_far(far, lower, position, highs, lows):
    branches, channels, _ = highs.shape
    half = branches // 2
    for j, piece in enumerate(far):
        uppers = piece.shape[0]
        count = channels // (uppers * lower)
        which = range(half) if j < 2 else range(half, branches)

        def block(u, i, piece=piece, which=which, count=count):
            at = (i - which[0]) * count
            return piece[u, at : at + count, :]

        join(6 + j % 2, lower, position, uppers, count, which, block, highs, lows)


def stack_kernel(*refs):
    pieces, (out, sem) = refs[:-2], refs[-2:]
    copies = [begin(piece, out.at[i], sem.at[i]) for i, piece in enumerate(pieces)]
    for copy in copies:
        copy.wait()


def stack(*pieces):
    n = len(pieces)
    out = jax.ShapeDtypeStruct((n,) + pieces[0].shape, F32)
    work = pl.CostEstimate(flops=0, bytes_accessed=8 * n * pieces[0].size, transcendentals=0)
    return call(stack_kernel, (out,), pieces, [], n, work, apart=range(n))[0]


def table_rows(table):
    return -(-table.shape[1] * table.shape[2] // 8) * 8


def pack_kernel(one, two, table, out, sem):
    parts, branches, count, lanes = table.shape
    rows = (out.shape[1] - table_rows(table)) // 2
    copies = []
    for i, piece in enumerate((one, two)):
        source = piece.at[:, pl.ds(0, rows)]
        copies.append(begin(source, out.at[:, pl.ds(i * rows, rows)], sem.at[i]))
    for n in range(branches):
        row = 2 * rows + n * count
        for p in range(parts):
            out[0, row : row + count, p * lanes : (p + 1) * lanes] = table[p, n]
    for copy in copies:
        copy.wait()


def pack(one, two, table, rows):
    uppers, _, channels = one.shape
    out = jax.ShapeDtypeStruct((uppers, 2 * rows + table_rows(table), channels), F32)
    work = pl.CostEstimate(flops=0, bytes_accessed=16 * one.size, transcendentals=0)
    return call(pack_kernel, (out,), (one, two, table), [], 2, work)[0]


def next_kernel(lower, position, near, near_core, far, far_core, highs, lows, table, _):
    branches, channels, _ = highs.shape
    _, uppers, _, count, _ = near.shape
    for core, (near_blocks, far_blocks) in enumerate(((near, far), (near_core, far_core))):
        for j in range(3):
            block = lambda u, i: near_blocks[j, u, i]
            join(2 * j + core, lower, position[0], uppers, count, range(branches), block, highs, lows)
        block = lambda u, i: far_blocks[u, i * count : (i + 1) * count, :]
        join(6 + core, lower, position[0], uppers, count, range(branches), block, highs, lows)
    parts, _, taps, lanes = table.shape
    for n in range(branches):
        row = branches * count + n * taps
        for p in range(parts):
            table[p, n] = far[0, row : row + taps, p * lanes : (p + 1) * lanes]


def next_part(position, near, near_core, far, far_core, like, lower):
    table, highs, lows = (jax.ShapeDtypeStruct(w.shape, w.dtype) for w in like)
    work = pl.CostEstimate(flops=0, bytes_accessed=16 * near.size, transcendentals=0)
    operands = (position, near, near_core, far, far_core)
    kernel = functools.partial(next_kernel, lower)
    highs, lows, table = call(kernel, (highs, lows, table), operands, [], 1, work)
    return table, highs, lows


def ahead_kernel(position, newest, pair, highs, lows, *refs):
    taps, (out, table, earlier, sem) = refs[:2], refs[2:]
    load = begin(pair.at[0], earlier, sem.at[0])
    chip = position[0] // 2
    for j, part in enumerate(taps):
        for n in range(part.shape[0]):
            table[chip ^ j, n] = part[n]
    blocks = [chip // 2]
    total = separable(newest, table, highs, lows, 0, blocks)
    load.wait()
    out[...] = total + separable(earlier, table, highs, lows, 1, blocks)


def ahead_part(position, newest, pair, matrices, taps):
    shape, channels = newest.shape, newest.shape[-1]
    table = (channels // LANES,) + taps[0].shape
    return call(
        ahead_kernel,
        (jax.ShapeDtypeStruct(shape, F32),),
        (position, newest, pair, *matrices, *taps),
        [(table, F32), (shape, F32)],
        1,
        cost(shape, 1),
        apart=(2,),
    )[0]


def first_kernel(n_far, n_taps, n_sums, lower, position, newest, pair, highs_in, lows_in, *refs):
    far, taps, refs = refs[:n_far], refs[n_far : n_far + n_taps], refs[n_far + n_taps :]
    sums, (out, highs, lows, table, earlier, first, second, sem) = refs[:n_sums], refs[n_sums:]
    load = begin(pair.at[0], earlier, sem.at[0])
    branches, channels, _ = highs.shape
    chip = position[0] // 2
    if n_taps == 1:
        table[...] = taps[0][...]
    else:
        below = far[2]
        for j, part in enumerate(taps):
            row = below.shape[1] - (n_taps - j) * TAP_ROWS
            for n in range(branches):
                table[chip ^ j, n] = part[n]
                lanes = slice(n * LANES, (n + 1) * LANES)
                table[chip ^ (j + 2), n] = below[0, row : row + 9, lanes]
    join_far(far, lower, position[0], highs, lows)
    blocks = [1 - chip // 2] if sums else None
    total = separable(newest, table, highs, lows, 0, blocks)
    for part in sums:
        total = total + part[...]
    first[...] = total
    load.wait()
    first[...] += separable(earlier, table, highs, lows, 1, blocks)
    second[...] = separable(first, table, highs, lows, 2) + newest[...]
    out[...] = separable(second, table, highs, lows, 3) + first[...]


def first_part(position, newest, pair, matrices, far, lower, taps, sums):
    shape, channels = newest.shape, newest.shape[-1]
    branches = matrices[0].shape[0]
    lanes = min(LANES, channels)
    like = [jax.ShapeDtypeStruct(m.shape, m.dtype) for m in matrices]
    return call(
        functools.partial(first_kernel, len(far), len(taps), len(sums), lower),
        (
            jax.ShapeDtypeStruct(shape, F32),
            *like,
            jax.ShapeDtypeStruct((channels // lanes, branches, 9, lanes), F32),
        ),
        (position, newest, pair, *matrices, *far, *taps, *sums),
        [(shape, F32)] * 3,
        1,
        cost(shape, 4),
        apart=(2,),
        aliases={3: 1, 4: 2},
    )


def doubled(x, axis, bit, dim):
    other = swap(x, axis, bit)
    upper = (lax.axis_index(axis) & bit) != 0
    return jnp.where(upper, jnp.concatenate([other, x], dim), jnp.concatenate([x, other], dim))


def near_taps(taps, axis):
    size = lax.axis_size(axis)
    branches, count, width = taps.shape
    if size == 8 and 2 * width == LANES:
        return doubled(taps, axis, 1, 2)
    if size & (size - 1):
        taps = lax.all_gather(taps, axis, axis=2, tiled=True)
    else:
        bit = 1
        while bit < size:
            taps = doubled(taps, axis, bit, 2)
            bit *= 2
    channels = taps.shape[-1]
    lanes = min(LANES, channels)
    taps = taps.reshape(branches, count, channels // lanes, lanes)
    return taps.transpose(2, 0, 1, 3)


def from_neighbours(shard, axis):
    shard = shard[None]
    bit = 8
    while bit < lax.axis_size(axis):
        shard = doubled(shard, axis, bit, 0)
        bit *= 2
    return shard, swap(shard, axis, 2), swap(shard, axis, 4)


def body(pair, stems, taps, matrices):
    section = lax.axis_index("section").astype(jnp.int32).reshape(1)
    position = lax.axis_index("dp").astype(jnp.int32).reshape(1)
    stems = stems[:, 0]
    ticks = stems.shape[0] + 1
    pair = pair[0, :, 0]
    shard = matrices[0]
    newest = pair[1]
    size = lax.axis_size("dp")
    simple = size & (size - 1) or size < 8
    lower = 1 if simple else 8
    taps = near_taps(after(taps[0], section, position), "dp")
    newest, taps = lax.optimization_barrier((newest, taps))
    taps = (taps, swap(taps, "dp", 2)) if taps.ndim == 3 else (taps,)
    passed_on = from_behind(newest, "section", around=True)
    far = sums = ()
    channels = newest.shape[-1]
    if simple:
        partial = near_part(position, {0: lax.all_gather(shard, "dp")}, lower)
    else:
        own, x, y = from_neighbours(shard, "dp")
        near = {0: own, 1: swap(own, "dp", 1), 2: x, 4: y}
        two = half_of(after(x, near[1]), 1, *(taps if len(taps) > 1 else ()))
        one = half_of(y, 0)
        x_late, y_late = after(x, two), after(y, one)
        near.update({3: swap(x_late, "dp", 1), 5: swap(y_late, "dp", 1)})
        one, two = swap(one, "dp", 2), swap(two, "dp", 4)
        partial = near_part(position, near, lower)
        if len(taps) > 1 and channels == 2 * DEPTH:
            sums = (ahead_part(after(position, passed_on), newest, pair, partial, taps),)
        one, two, *_ = lax.optimization_barrier((one, two, passed_on, *partial, *sums))
        far = (one, swap(one, "dp", 1), two, swap(two, "dp", 1))
    output, *weights, table = first_part(
        position, newest, pair, partial, far, lower, taps, sums
    )
    weights = (table, *weights)

    if simple:
        next_shard = lax.all_gather(from_ahead(shard, "section"), "dp")
        next_weights = (from_ahead(table, "section"), *near_part(position, {0: next_shard}, lower))
    else:
        near = lax.optimization_barrier((own, x, y, *partial))[:3]
        next_near = from_ahead(stack(*near), "section")
        rows = far[0].shape[1]
    emitted = None
    held = (1, 0, newest)
    for tick in range(1, ticks - 1):
        earlier, newest, past = passed_on, from_behind(output, "section"), output
        if tick > 1:
            earlier = after(earlier, output)
        passed_on = from_behind(newest, "section", 1)
        early = early_part(tick, min(tick, 2), section, stems, earlier, weights)
        if tick == 1 and not simple:
            next_far = from_ahead(pack(after(far[0], early), far[2], table, rows), "section")
        emitted, output = late_part(
            tick, 1, section, stems, newest, early, weights, past, emitted, 12 if tick > 1 else 2
        )
        held = (tick, 1, newest)
        last_early = early

    if not simple:
        next_near, next_far, _ = lax.optimization_barrier((next_near, next_far, last_early))
        blocks = next_near, swap(next_near, "dp", 1), next_far, swap(next_far, "dp", 1)
        next_weights = next_part(position, *blocks, weights, lower)
    emitted, ahead = last_cell(
        held[0], held[1], section, stems, held[2], output, next_weights, emitted
    )
    got = from_behind(ahead, "section")
    emitted = last_part(section, got, stem_part(stems, weights), emitted)
    return emitted[None, :, None]


def solution(mesh):
    placed = (
        P("section", None, "dp", None, None, None),
        P(None, "dp", None, None, None),
        P("section", None, None, "dp"),
        P("section", None, "dp", None),
    )
    return jax.shard_map(
        body,
        mesh=mesh,
        in_specs=placed,
        out_specs=P("section", None, "dp", None, None, None),
        check_vma=False,
    )
```

```python
import functools

import jax
import jax.numpy as jnp
from jax import lax
from jax.experimental import pallas as pl
from jax.experimental.pallas import tpu as pltpu
from jax.sharding import PartitionSpec as P

F32 = jnp.float32
BF16 = jnp.bfloat16
VMEM_LIMIT = 16 * 1024 * 1024
LANES = 128
DEPTH = 256


def swap(x, axis, bit):
    size = lax.axis_size(axis)
    return lax.ppermute(x, axis, [(i, i ^ bit) for i in range(size)])


def from_behind(x, axis, first=0, around=False):
    size = lax.axis_size(axis)
    pairs = [(i, i + 1) for i in range(first, size - 1)]
    return lax.ppermute(x, axis, pairs + [(size - 1, 0)] * (around and size > 1))


def from_ahead(x, axis):
    return lax.ppermute(x, axis, [(i + 1, i) for i in range(lax.axis_size(axis) - 1)])


def after(x, *others):
    return lax.optimization_barrier((x, *others))[0]


def begin(source, target, sem):
    copy = pltpu.make_async_copy(source, target, sem)
    copy.start()
    return copy


def split(x):
    high = x.astype(BF16)
    return high, (x - high.astype(F32)).astype(BF16)


def call(kernel, outs, operands, scratch, copies, cost, apart=(), outs_apart=(), aliases=None, limit=VMEM_LIMIT):
    def spec(x, i, apart):
        space = pl.ANY if i in apart else pltpu.SMEM if x.dtype == jnp.int32 else pltpu.VMEM
        return pl.BlockSpec(memory_space=space)

    return pl.pallas_call(
        kernel,
        out_shape=outs,
        in_specs=[spec(x, i, apart) for i, x in enumerate(operands)],
        out_specs=tuple(spec(x, i, outs_apart) for i, x in enumerate(outs)),
        scratch_shapes=[pltpu.VMEM(*s) for s in scratch] + [pltpu.SemaphoreType.DMA((copies,))],
        input_output_aliases=aliases or {},
        compiler_params=pltpu.CompilerParams(vmem_limit_bytes=limit),
        cost_estimate=cost,
    )(*operands)


def cost(shape, convolutions):
    rows, columns, channels = shape
    size = rows * columns * channels
    return pl.CostEstimate(
        flops=6 * convolutions * size * channels,
        bytes_accessed=4 * (3 * size + convolutions * channels * channels),
        transcendentals=0,
    )


def shifted(u, by):
    side = u.shape[1]
    column = lax.broadcasted_iota(jnp.int32, u.shape, 1)
    outside = 0 if by == 1 else side - 1
    return jnp.where(column == outside, 0.0, pltpu.roll(u, by % side, 1))


def depthwise(source, table, branch, part, width):
    low = part * width
    if not isinstance(part, int):
        low = pl.multiple_of(low, width)
    x = jnp.maximum(source[:, :, pl.ds(low, width)], 0.0)
    nothing = jnp.zeros((1,) + x.shape[1:], F32)
    above = jnp.concatenate([nothing, x[:-1]], 0)
    below = jnp.concatenate([x[1:], nothing], 0)
    tap = [table[part, branch, k : k + 1, :].reshape(1, 1, width) for k in range(9)]
    by_column = [above * tap[j] + x * tap[3 + j] + below * tap[6 + j] for j in range(3)]
    return shifted(by_column[0], 1) + by_column[1] + shifted(by_column[2], -1)


def separable(source, table, highs, lows, branch, blocks=None):
    rows, columns, channels = source.shape
    width = min(LANES, channels)
    depth = min(DEPTH, channels)
    each = depth // width
    total = None
    for block in range(channels // depth) if blocks is None else blocks:
        mixed_in = []
        for i in range(each):
            value = depthwise(source, table, branch, block * each + i, width)
            mixed_in.append(split(value.reshape(rows * columns, width)))
        high = jnp.concatenate([p[0] for p in mixed_in], 1)
        low = jnp.concatenate([p[1] for p in mixed_in], 1)
        k = block * depth
        if not isinstance(block, int):
            k = pl.multiple_of(k, depth)
        matrix_high = highs[branch, pl.ds(k, depth), :]
        matrix_low = lows[branch, pl.ds(k, depth), :]
        both = jnp.concatenate([high, low], 0)
        product = jnp.dot(both, matrix_high, preferred_element_type=F32)
        product = product[: high.shape[0]] + product[high.shape[0] :]
        product = product + jnp.dot(high, matrix_low, preferred_element_type=F32)
        total = product if total is None else total + product
    return total.reshape(source.shape)


def fetch(tick, at, section, stems, got, held, sem):
    for s in range(at):

        @pl.when(section == s)
        def _(s=s):
            begin(stems.at[tick - 1 - s], held, sem)

    @pl.when(section >= at)
    def _():
        begin(got, held, sem)

    return pltpu.make_async_copy(got, held, sem)


def early_kernel(tick, at, section, stems, got, table, highs, lows, out, held, sem):
    fetch(tick, at, section[0], stems, got, held, sem.at[0]).wait()
    out[...] = separable(held, table, highs, lows, 1)


def late_kernel(tick, at, section, stems, got, early, table, highs, lows, past, *rest):
    emitted, out, newest, first, second, sem = rest[-6:]
    store = begin(past, emitted.at[tick - 1], sem.at[1])
    fetch(tick, at, section[0], stems, got, newest, sem.at[0]).wait()
    first[...] = separable(newest, table, highs, lows, 0) + early[...]
    second[...] = separable(first, table, highs, lows, 2) + newest[...]
    out[...] = separable(second, table, highs, lows, 3) + first[...]
    store.wait()


def early_part(tick, at, section, stems, got, weights):
    shape = got.shape
    return call(
        functools.partial(early_kernel, tick, at),
        (jax.ShapeDtypeStruct(shape, F32),),
        (section, stems, got, *weights),
        [(shape, F32)],
        1,
        cost(shape, 1),
        apart=(1, 2),
    )[0]


def late_part(tick, at, section, stems, got, early, weights, past, emitted, weight=2):
    shape = got.shape
    whole = jax.ShapeDtypeStruct((stems.shape[0] + 1,) + shape, F32)
    operands = (section, stems, got, early, *weights, past)
    return call(
        functools.partial(late_kernel, tick, at),
        (whole, jax.ShapeDtypeStruct(shape, F32)),
        operands if emitted is None else operands + (emitted,),
        [(shape, F32)] * 3,
        2,
        cost(shape, 3 * weight),
        apart=(1, 2, 8),
        outs_apart=(0,),
        aliases=None if emitted is None else {8: 0},
    )


def last_cell_kernel(tick, at, section, stems, got, newest, table, highs, lows, _, *rest):
    emitted, out, earlier, first, second, sem = rest
    load = fetch(tick, at, section[0], stems, got, earlier, sem.at[0])
    store = begin(newest, emitted.at[tick], sem.at[1])
    first[...] = separable(newest, table, highs, lows, 0)
    load.wait()
    first[...] += separable(earlier, table, highs, lows, 1)
    second[...] = separable(first, table, highs, lows, 2) + newest[...]
    out[...] = separable(second, table, highs, lows, 3) + first[...]
    store.wait()


def last_cell(tick, at, section, stems, got, newest, weights, emitted):
    shape = got.shape
    whole = jax.ShapeDtypeStruct(emitted.shape, F32)
    return call(
        functools.partial(last_cell_kernel, tick, at),
        (whole, jax.ShapeDtypeStruct(shape, F32)),
        (section, stems, got, newest, *weights, emitted),
        [(shape, F32)] * 3,
        2,
        cost(shape, 7),
        apart=(1, 2, 7),
        outs_apart=(0,),
        aliases={7: 0},
    )


def stem_kernel(stems, table, highs, lows, out, held, first, second, sem):
    begin(stems.at[stems.shape[0] - 1], held, sem.at[0]).wait()
    first[...] = separable(held, table, highs, lows, 0)
    first[...] += separable(held, table, highs, lows, 1)
    second[...] = separable(first, table, highs, lows, 2) + held[...]
    out[...] = separable(second, table, highs, lows, 3) + first[...]


def stem_part(stems, weights):
    shape = stems.shape[1:]
    a_map = jax.ShapeDtypeStruct(shape, F32)
    scratch = [(shape, F32)] * 3
    operands = (stems, *weights)
    return call(stem_kernel, (a_map,), operands, scratch, 1, cost(shape, 4), apart=(0,))[0]


def last_kernel(section, got, own, _, emitted, sem):
    target = emitted.at[emitted.shape[0] - 1]

    @pl.when(section[0] == 0)
    def _():
        begin(own, target, sem.at[0])

    @pl.when(section[0] > 0)
    def _():
        begin(got, target, sem.at[0])

    pltpu.make_async_copy(got, target, sem.at[0]).wait()


def last_part(section, got, own, emitted):
    whole = jax.ShapeDtypeStruct(emitted.shape, F32)
    work = pl.CostEstimate(flops=0, bytes_accessed=8 * got.size, transcendentals=0)
    operands = (section, got, own, emitted)
    return call(
        last_kernel, (whole,), operands, [], 1, work, apart=(3,), outs_apart=(0,), aliases={3: 0}
    )[0]


def join(key, lower, position, uppers, count, branches, block, highs, lows):
    for u in range(uppers):
        at = u * lower + ((position & (lower - 1)) ^ key)
        row = pl.multiple_of(at * count, count)
        for i in branches:
            high, low = split(block(u, i))
            highs[i, pl.ds(row, count), :] = high
            lows[i, pl.ds(row, count), :] = low


def near_kernel(keys, lower, position, *refs):
    pieces, (highs, lows, _) = refs[:-3], refs[-3:]
    for key, piece in zip(keys, pieces):
        uppers, branches, count, _ = piece.shape
        block = lambda u, i, piece=piece: piece[u, i]
        join(key, lower, position[0], uppers, count, range(branches), block, highs, lows)


def near_part(position, blocks, lower):
    uppers, branches, _, channels = blocks[0].shape
    matrices = jax.ShapeDtypeStruct((branches, channels, channels), BF16)
    return call(
        functools.partial(near_kernel, list(blocks), lower),
        (matrices, matrices),
        (position, *blocks.values()),
        [],
        1,
        pl.CostEstimate(flops=0, bytes_accessed=8 * matrices.size, transcendentals=0),
    )


def half_kernel(start, block, *refs):
    taps, (out, sem) = refs[:-2], refs[-2:]
    uppers, branches, count, _ = block.shape
    half = branches // 2
    copies = []
    for u in range(uppers):
        for i in range(half):
            target = out.at[u, pl.ds(i * count, count)]
            copies.append(begin(block.at[u, start + i], target, sem.at[u * half + i]))
    for j, chip in enumerate(taps):
        row = half * count + j * chip.shape[1]
        for n in range(branches):
            out[0, row : row + 9, n * LANES : (n + 1) * LANES] = chip[n]
    for copy in copies:
        copy.wait()


def half_of(block, start, *taps):
    uppers, branches, count, channels = block.shape
    half = branches // 2
    extra = -(-sum(chip.shape[1] for chip in taps) // 8) * 8
    out = jax.ShapeDtypeStruct((uppers, half * count + extra, channels), F32)
    work = pl.CostEstimate(flops=0, bytes_accessed=4 * block.size, transcendentals=0)
    kernel = functools.partial(half_kernel, start * half)
    return call(kernel, (out,), (block, *taps), [], half * uppers, work)[0]


def join_far(far, lower, position, highs, lows):
    branches, channels, _ = highs.shape
    half = branches // 2
    for j, piece in enumerate(far):
        uppers = piece.shape[0]
        count = channels // (uppers * lower)
        which = range(half) if j < 2 else range(half, branches)

        def block(u, i, piece=piece, which=which, count=count):
            at = (i - which[0]) * count
            return piece[u, at : at + count, :]

        join(6 + j % 2, lower, position, uppers, count, which, block, highs, lows)


def stack_kernel(*refs):
    pieces, (out, sem) = refs[:-2], refs[-2:]
    copies = [begin(piece, out.at[i], sem.at[i]) for i, piece in enumerate(pieces)]
    for copy in copies:
        copy.wait()


def stack(*pieces):
    n = len(pieces)
    out = jax.ShapeDtypeStruct((n,) + pieces[0].shape, F32)
    work = pl.CostEstimate(flops=0, bytes_accessed=8 * n * pieces[0].size, transcendentals=0)
    return call(stack_kernel, (out,), pieces, [], n, work, apart=range(n))[0]


def table_rows(table):
    return -(-table.shape[1] * table.shape[2] // 8) * 8


def pack_kernel(one, two, table, out, sem):
    parts, branches, count, lanes = table.shape
    rows = (out.shape[1] - table_rows(table)) // 2
    copies = []
    for i, piece in enumerate((one, two)):
        source = piece.at[:, pl.ds(0, rows)]
        copies.append(begin(source, out.at[:, pl.ds(i * rows, rows)], sem.at[i]))
    for n in range(branches):
        row = 2 * rows + n * count
        for p in range(parts):
            out[0, row : row + count, p * lanes : (p + 1) * lanes] = table[p, n]
    for copy in copies:
        copy.wait()


def pack(one, two, table, rows):
    uppers, _, channels = one.shape
    out = jax.ShapeDtypeStruct((uppers, 2 * rows + table_rows(table), channels), F32)
    work = pl.CostEstimate(flops=0, bytes_accessed=16 * one.size, transcendentals=0)
    return call(pack_kernel, (out,), (one, two, table), [], 2, work)[0]


def next_kernel(lower, position, near, near_core, far, far_core, highs, lows, table, _):
    branches, channels, _ = highs.shape
    _, uppers, _, count, _ = near.shape
    for core, (near_blocks, far_blocks) in enumerate(((near, far), (near_core, far_core))):
        for j in range(3):
            block = lambda u, i: near_blocks[j, u, i]
            join(2 * j + core, lower, position[0], uppers, count, range(branches), block, highs, lows)
        block = lambda u, i: far_blocks[u, i * count : (i + 1) * count, :]
        join(6 + core, lower, position[0], uppers, count, range(branches), block, highs, lows)
    parts, _, taps, lanes = table.shape
    for n in range(branches):
        row = branches * count + n * taps
        for p in range(parts):
            table[p, n] = far[0, row : row + taps, p * lanes : (p + 1) * lanes]


def next_part(position, near, near_core, far, far_core, like, lower):
    table, highs, lows = (jax.ShapeDtypeStruct(w.shape, w.dtype) for w in like)
    work = pl.CostEstimate(flops=0, bytes_accessed=16 * near.size, transcendentals=0)
    operands = (position, near, near_core, far, far_core)
    kernel = functools.partial(next_kernel, lower)
    highs, lows, table = call(kernel, (highs, lows, table), operands, [], 1, work)
    return table, highs, lows


def ahead_kernel(position, newest, pair, highs, lows, *refs):
    taps, (out, table, earlier, sem) = refs[:2], refs[2:]
    load = begin(pair.at[0], earlier, sem.at[0])
    chip = position[0] // 2
    for j, part in enumerate(taps):
        for n in range(part.shape[0]):
            table[chip ^ j, n] = part[n]
    blocks = [chip // 2]
    total = separable(newest, table, highs, lows, 0, blocks)
    load.wait()
    out[...] = total + separable(earlier, table, highs, lows, 1, blocks)


def ahead_part(position, newest, pair, matrices, taps):
    shape, channels = newest.shape, newest.shape[-1]
    table = (channels // LANES,) + taps[0].shape
    return call(
        ahead_kernel,
        (jax.ShapeDtypeStruct(shape, F32),),
        (position, newest, pair, *matrices, *taps),
        [(table, F32), (shape, F32)],
        1,
        cost(shape, 1),
        apart=(2,),
    )[0]


def first_kernel(n_far, n_taps, n_sums, lower, position, newest, pair, highs_in, lows_in, *refs):
    far, taps, refs = refs[:n_far], refs[n_far : n_far + n_taps], refs[n_far + n_taps :]
    sums, (out, highs, lows, table, earlier, first, second, sem) = refs[:n_sums], refs[n_sums:]
    load = begin(pair.at[0], earlier, sem.at[0])
    branches, channels, _ = highs.shape
    chip = position[0] // 2
    if n_taps == 1:
        table[...] = taps[0][...]
    else:
        below = far[2]
        for j, part in enumerate(taps):
            row = far[0].shape[1] + j * part.shape[1]
            for n in range(branches):
                table[chip ^ j, n] = part[n]
                lanes = slice(n * LANES, (n + 1) * LANES)
                table[chip ^ (j + 2), n] = below[0, row : row + 9, lanes]
    join_far(far, lower, position[0], highs, lows)
    blocks = [1 - chip // 2] if sums else None
    total = separable(newest, table, highs, lows, 0, blocks)
    for part in sums:
        total = total + part[...]
    first[...] = total
    load.wait()
    first[...] += separable(earlier, table, highs, lows, 1, blocks)
    second[...] = separable(first, table, highs, lows, 2) + newest[...]
    out[...] = separable(second, table, highs, lows, 3) + first[...]


def first_part(position, newest, pair, matrices, far, lower, taps, sums):
    shape, channels = newest.shape, newest.shape[-1]
    branches = matrices[0].shape[0]
    lanes = min(LANES, channels)
    like = [jax.ShapeDtypeStruct(m.shape, m.dtype) for m in matrices]
    return call(
        functools.partial(first_kernel, len(far), len(taps), len(sums), lower),
        (
            jax.ShapeDtypeStruct(shape, F32),
            *like,
            jax.ShapeDtypeStruct((channels // lanes, branches, 9, lanes), F32),
        ),
        (position, newest, pair, *matrices, *far, *taps, *sums),
        [(shape, F32)] * 3,
        1,
        cost(shape, 4),
        apart=(2,),
        aliases={3: 1, 4: 2},
    )


def doubled(x, axis, bit, dim):
    other = swap(x, axis, bit)
    upper = (lax.axis_index(axis) & bit) != 0
    return jnp.where(upper, jnp.concatenate([other, x], dim), jnp.concatenate([x, other], dim))


def near_taps(taps, axis):
    size = lax.axis_size(axis)
    branches, count, width = taps.shape
    if size == 8 and 2 * width == LANES:
        return doubled(taps, axis, 1, 2)
    if size & (size - 1):
        taps = lax.all_gather(taps, axis, axis=2, tiled=True)
    else:
        bit = 1
        while bit < size:
            taps = doubled(taps, axis, bit, 2)
            bit *= 2
    channels = taps.shape[-1]
    lanes = min(LANES, channels)
    taps = taps.reshape(branches, count, channels // lanes, lanes)
    return taps.transpose(2, 0, 1, 3)


def from_neighbours(shard, axis):
    shard = shard[None]
    bit = 8
    while bit < lax.axis_size(axis):
        shard = doubled(shard, axis, bit, 0)
        bit *= 2
    return shard, swap(shard, axis, 2), swap(shard, axis, 4)


def body(pair, stems, taps, matrices):
    section = lax.axis_index("section").astype(jnp.int32).reshape(1)
    position = lax.axis_index("dp").astype(jnp.int32).reshape(1)
    stems = stems[:, 0]
    ticks = stems.shape[0] + 1
    pair = pair[0, :, 0]
    shard = matrices[0]
    newest = pair[1]
    size = lax.axis_size("dp")
    simple = size & (size - 1) or size < 8
    lower = 1 if simple else 8
    taps = near_taps(after(taps[0], section, position), "dp")
    newest, taps = lax.optimization_barrier((newest, taps))
    taps = (taps, swap(taps, "dp", 2)) if taps.ndim == 3 else (taps,)
    passed_on = from_behind(newest, "section", around=True)
    far = sums = ()
    channels = newest.shape[-1]
    if simple:
        partial = near_part(position, {0: lax.all_gather(shard, "dp")}, lower)
    else:
        own, x, y = from_neighbours(shard, "dp")
        near = {0: own, 1: swap(own, "dp", 1), 2: x, 4: y}
        two = half_of(after(x, near[1]), 1, *(taps if len(taps) > 1 else ()))
        one = half_of(y, 0)
        x_late, y_late = after(x, two), after(y, one)
        near.update({3: swap(x_late, "dp", 1), 5: swap(y_late, "dp", 1)})
        one, two = swap(one, "dp", 2), swap(two, "dp", 4)
        partial = near_part(position, near, lower)
        if len(taps) > 1 and channels == 2 * DEPTH:
            sums = (ahead_part(after(position, passed_on), newest, pair, partial, taps),)
        one, two, *_ = lax.optimization_barrier((one, two, passed_on, *partial, *sums))
        far = (one, swap(one, "dp", 1), two, swap(two, "dp", 1))
    output, *weights, table = first_part(
        position, newest, pair, partial, far, lower, taps, sums
    )
    weights = (table, *weights)

    if simple:
        next_shard = lax.all_gather(from_ahead(shard, "section"), "dp")
        next_weights = (from_ahead(table, "section"), *near_part(position, {0: next_shard}, lower))
    else:
        near = lax.optimization_barrier((own, x, y, *partial))[:3]
        next_near = from_ahead(stack(*near), "section")
        rows = far[0].shape[1]
    emitted = None
    held = (1, 0, newest)
    for tick in range(1, ticks - 1):
        earlier, newest, past = passed_on, from_behind(output, "section"), output
        if tick > 1:
            earlier = after(earlier, output)
        passed_on = from_behind(newest, "section", 1)
        early = early_part(tick, min(tick, 2), section, stems, earlier, weights)
        if tick == 1 and not simple:
            next_far = from_ahead(pack(after(far[0], early), far[2], table, rows), "section")
        emitted, output = late_part(
            tick, 1, section, stems, newest, early, weights, past, emitted, 12 if tick > 1 else 2
        )
        held = (tick, 1, newest)
        last_early = early

    if not simple:
        next_near, next_far, _ = lax.optimization_barrier((next_near, next_far, last_early))
        blocks = next_near, swap(next_near, "dp", 1), next_far, swap(next_far, "dp", 1)
        next_weights = next_part(position, *blocks, weights, lower)
    emitted, ahead = last_cell(
        held[0], held[1], section, stems, held[2], output, next_weights, emitted
    )
    got = from_behind(ahead, "section")
    emitted = last_part(section, got, stem_part(stems, weights), emitted)
    return emitted[None, :, None]


def solution(mesh):
    placed = (
        P("section", None, "dp", None, None, None),
        P(None, "dp", None, None, None),
        P("section", None, None, "dp"),
        P("section", None, "dp", None),
    )
    return jax.shard_map(
        body,
        mesh=mesh,
        in_specs=placed,
        out_specs=P("section", None, "dp", None, None, None),
        check_vma=False,
    )
```

```python
import functools

import jax
import jax.numpy as jnp
from jax import lax
from jax.experimental import pallas as pl
from jax.experimental.pallas import tpu as pltpu
from jax.sharding import PartitionSpec as P

F32 = jnp.float32
BF16 = jnp.bfloat16
VMEM_LIMIT = 16 * 1024 * 1024
LANES = 128
DEPTH = 256
TAP_ROWS = 16


def swap(x, axis, bit):
    size = lax.axis_size(axis)
    return lax.ppermute(x, axis, [(i, i ^ bit) for i in range(size)])


def from_behind(x, axis, first=0, around=False):
    size = lax.axis_size(axis)
    pairs = [(i, i + 1) for i in range(first, size - 1)]
    return lax.ppermute(x, axis, pairs + [(size - 1, 0)] * (around and size > 1))


def from_ahead(x, axis):
    return lax.ppermute(x, axis, [(i + 1, i) for i in range(lax.axis_size(axis) - 1)])


def after(x, *others):
    return lax.optimization_barrier((x, *others))[0]


def begin(source, target, sem):
    copy = pltpu.make_async_copy(source, target, sem)
    copy.start()
    return copy


def split(x):
    high = x.astype(BF16)
    return high, (x - high.astype(F32)).astype(BF16)


def call(kernel, outs, operands, scratch, copies, cost, apart=(), outs_apart=(), aliases=None, limit=VMEM_LIMIT):
    def spec(x, i, apart):
        space = pl.ANY if i in apart else pltpu.SMEM if x.dtype == jnp.int32 else pltpu.VMEM
        return pl.BlockSpec(memory_space=space)

    return pl.pallas_call(
        kernel,
        out_shape=outs,
        in_specs=[spec(x, i, apart) for i, x in enumerate(operands)],
        out_specs=tuple(spec(x, i, outs_apart) for i, x in enumerate(outs)),
        scratch_shapes=[pltpu.VMEM(*s) for s in scratch] + [pltpu.SemaphoreType.DMA((copies,))],
        input_output_aliases=aliases or {},
        compiler_params=pltpu.CompilerParams(vmem_limit_bytes=limit),
        cost_estimate=cost,
    )(*operands)


def cost(shape, convolutions):
    rows, columns, channels = shape
    size = rows * columns * channels
    return pl.CostEstimate(
        flops=6 * convolutions * size * channels,
        bytes_accessed=4 * (3 * size + convolutions * channels * channels),
        transcendentals=0,
    )


def shifted(u, by):
    side = u.shape[1]
    column = lax.broadcasted_iota(jnp.int32, u.shape, 1)
    outside = 0 if by == 1 else side - 1
    return jnp.where(column == outside, 0.0, pltpu.roll(u, by % side, 1))


def depthwise(source, table, branch, part, width):
    low = part * width
    if not isinstance(part, int):
        low = pl.multiple_of(low, width)
    x = jnp.maximum(source[:, :, pl.ds(low, width)], 0.0)
    nothing = jnp.zeros((1,) + x.shape[1:], F32)
    above = jnp.concatenate([nothing, x[:-1]], 0)
    below = jnp.concatenate([x[1:], nothing], 0)
    tap = [table[part, branch, k : k + 1, :].reshape(1, 1, width) for k in range(9)]
    by_column = [above * tap[j] + x * tap[3 + j] + below * tap[6 + j] for j in range(3)]
    return shifted(by_column[0], 1) + by_column[1] + shifted(by_column[2], -1)


def separable(source, table, highs, lows, branch, blocks=None, loads=()):
    rows, columns, channels = source.shape
    width = min(LANES, channels)
    depth = min(DEPTH, channels)
    each = depth // width
    total = None
    for block in range(channels // depth) if blocks is None else blocks:
        if loads:
            loads[block].wait()
        mixed_in = []
        for i in range(each):
            value = depthwise(source, table, branch, block * each + i, width)
            mixed_in.append(split(value.reshape(rows * columns, width)))
        high = jnp.concatenate([p[0] for p in mixed_in], 1)
        low = jnp.concatenate([p[1] for p in mixed_in], 1)
        k = block * depth
        if not isinstance(block, int):
            k = pl.multiple_of(k, depth)
        matrix_high = highs[branch, pl.ds(k, depth), :]
        matrix_low = lows[branch, pl.ds(k, depth), :]
        both = jnp.concatenate([high, low], 0)
        product = jnp.dot(both, matrix_high, preferred_element_type=F32)
        product = product[: high.shape[0]] + product[high.shape[0] :]
        product = product + jnp.dot(high, matrix_low, preferred_element_type=F32)
        total = product if total is None else total + product
    return total.reshape(source.shape)


def fetch(tick, at, section, stems, got, held, sem, lanes=slice(None)):
    for s in range(at):

        @pl.when(section == s)
        def _(s=s):
            begin(stems.at[tick - 1 - s, :, :, lanes], held.at[:, :, lanes], sem)

    @pl.when(section >= at)
    def _():
        begin(got.at[:, :, lanes], held.at[:, :, lanes], sem)

    return pltpu.make_async_copy(got.at[:, :, lanes], held.at[:, :, lanes], sem)


def early_kernel(tick, at, section, stems, got, table, highs, lows, out, held, sem):
    fetch(tick, at, section[0], stems, got, held, sem.at[0]).wait()
    out[...] = separable(held, table, highs, lows, 1)


def late_kernel(tick, at, section, stems, got, early, table, highs, lows, past, *rest):
    emitted, out, newest, first, second, sem = rest[-6:]
    store = begin(past, emitted.at[tick - 1], sem.at[sem.shape[0] - 1])
    channels = newest.shape[-1]
    depth = min(DEPTH, channels)
    loads = [
        fetch(tick, at, section[0], stems, got, newest, sem.at[i], pl.ds(i * depth, depth))
        for i in range(channels // depth)
    ]
    first[...] = separable(newest, table, highs, lows, 0, loads=loads) + early[...]
    second[...] = separable(first, table, highs, lows, 2) + newest[...]
    out[...] = separable(second, table, highs, lows, 3) + first[...]
    store.wait()


def early_part(tick, at, section, stems, got, weights):
    shape = got.shape
    return call(
        functools.partial(early_kernel, tick, at),
        (jax.ShapeDtypeStruct(shape, F32),),
        (section, stems, got, *weights),
        [(shape, F32)],
        1,
        cost(shape, 1),
        apart=(1, 2),
    )[0]


def late_part(tick, at, section, stems, got, early, weights, past, emitted, weight=2):
    shape = got.shape
    whole = jax.ShapeDtypeStruct((stems.shape[0] + 1,) + shape, F32)
    operands = (section, stems, got, early, *weights, past)
    return call(
        functools.partial(late_kernel, tick, at),
        (whole, jax.ShapeDtypeStruct(shape, F32)),
        operands if emitted is None else operands + (emitted,),
        [(shape, F32)] * 3,
        1 + shape[-1] // min(DEPTH, shape[-1]),
        cost(shape, 3 * weight),
        apart=(1, 2, 8),
        outs_apart=(0,),
        aliases=None if emitted is None else {8: 0},
    )


def last_cell_kernel(tick, at, section, stems, got, newest, table, highs, lows, _, *rest):
    emitted, out, earlier, first, second, sem = rest
    load = fetch(tick, at, section[0], stems, got, earlier, sem.at[0])
    store = begin(newest, emitted.at[tick], sem.at[1])
    first[...] = separable(newest, table, highs, lows, 0)
    load.wait()
    first[...] += separable(earlier, table, highs, lows, 1)
    second[...] = separable(first, table, highs, lows, 2) + newest[...]
    out[...] = separable(second, table, highs, lows, 3) + first[...]
    store.wait()


def last_cell(tick, at, section, stems, got, newest, weights, emitted):
    shape = got.shape
    whole = jax.ShapeDtypeStruct(emitted.shape, F32)
    return call(
        functools.partial(last_cell_kernel, tick, at),
        (whole, jax.ShapeDtypeStruct(shape, F32)),
        (section, stems, got, newest, *weights, emitted),
        [(shape, F32)] * 3,
        2,
        cost(shape, 7),
        apart=(1, 2, 7),
        outs_apart=(0,),
        aliases={7: 0},
    )


def stem_kernel(stems, table, highs, lows, out, held, first, second, sem):
    begin(stems.at[stems.shape[0] - 1], held, sem.at[0]).wait()
    first[...] = separable(held, table, highs, lows, 0)
    first[...] += separable(held, table, highs, lows, 1)
    second[...] = separable(first, table, highs, lows, 2) + held[...]
    out[...] = separable(second, table, highs, lows, 3) + first[...]


def stem_part(stems, weights):
    shape = stems.shape[1:]
    a_map = jax.ShapeDtypeStruct(shape, F32)
    scratch = [(shape, F32)] * 3
    operands = (stems, *weights)
    return call(stem_kernel, (a_map,), operands, scratch, 1, cost(shape, 4), apart=(0,))[0]


def last_kernel(section, got, own, _, emitted, sem):
    target = emitted.at[emitted.shape[0] - 1]

    @pl.when(section[0] == 0)
    def _():
        begin(own, target, sem.at[0])

    @pl.when(section[0] > 0)
    def _():
        begin(got, target, sem.at[0])

    pltpu.make_async_copy(got, target, sem.at[0]).wait()


def last_part(section, got, own, emitted):
    whole = jax.ShapeDtypeStruct(emitted.shape, F32)
    work = pl.CostEstimate(flops=0, bytes_accessed=8 * got.size, transcendentals=0)
    operands = (section, got, own, emitted)
    return call(
        last_kernel, (whole,), operands, [], 1, work, apart=(3,), outs_apart=(0,), aliases={3: 0}
    )[0]


def join(key, lower, position, uppers, count, branches, block, highs, lows):
    for u in range(uppers):
        at = u * lower + ((position & (lower - 1)) ^ key)
        row = pl.multiple_of(at * count, count)
        for i in branches:
            high, low = split(block(u, i))
            highs[i, pl.ds(row, count), :] = high
            lows[i, pl.ds(row, count), :] = low


def near_kernel(keys, lower, position, *refs):
    pieces, (highs, lows, _) = refs[:-3], refs[-3:]
    for key, piece in zip(keys, pieces):
        uppers, branches, count, _ = piece.shape
        block = lambda u, i, piece=piece: piece[u, i]
        join(key, lower, position[0], uppers, count, range(branches), block, highs, lows)


def near_part(position, blocks, lower):
    uppers, branches, _, channels = blocks[0].shape
    matrices = jax.ShapeDtypeStruct((branches, channels, channels), BF16)
    return call(
        functools.partial(near_kernel, list(blocks), lower),
        (matrices, matrices),
        (position, *blocks.values()),
        [],
        1,
        pl.CostEstimate(flops=0, bytes_accessed=8 * matrices.size, transcendentals=0),
    )


def half_kernel(start, block, *refs):
    taps, (out, sem) = refs[:-2], refs[-2:]
    uppers, branches, count, _ = block.shape
    half = branches // 2
    copies = []
    for u in range(uppers):
        for i in range(half):
            target = out.at[u, pl.ds(i * count, count)]
            copies.append(begin(block.at[u, start + i], target, sem.at[u * half + i]))
    for j, chip in enumerate(taps):
        row = half * count + j * TAP_ROWS
        for n in range(branches):
            out[0, row : row + 9, n * LANES : (n + 1) * LANES] = chip[n]
    for copy in copies:
        copy.wait()


def half_of(block, start, *taps):
    uppers, branches, count, channels = block.shape
    half = branches // 2
    out = jax.ShapeDtypeStruct((uppers, half * count + TAP_ROWS * len(taps), channels), F32)
    work = pl.CostEstimate(flops=0, bytes_accessed=4 * block.size, transcendentals=0)
    kernel = functools.partial(half_kernel, start * half)
    return call(kernel, (out,), (block, *taps), [], half * uppers, work)[0]


def join_far(far, lower, position, highs, lows):
    branches, channels, _ = highs.shape
    half = branches // 2
    for j, piece in enumerate(far):
        uppers = piece.shape[0]
        count = channels // (uppers * lower)
        which = range(half) if j < 2 else range(half, branches)

        def block(u, i, piece=piece, which=which, count=count):
            at = (i - which[0]) * count
            return piece[u, at : at + count, :]

        join(6 + j % 2, lower, position, uppers, count, which, block, highs, lows)


def stack_kernel(*refs):
    pieces, (out, sem) = refs[:-2], refs[-2:]
    copies = [begin(piece, out.at[i], sem.at[i]) for i, piece in enumerate(pieces)]
    for copy in copies:
        copy.wait()


def stack(*pieces):
    n = len(pieces)
    out = jax.ShapeDtypeStruct((n,) + pieces[0].shape, F32)
    work = pl.CostEstimate(flops=0, bytes_accessed=8 * n * pieces[0].size, transcendentals=0)
    return call(stack_kernel, (out,), pieces, [], n, work, apart=range(n))[0]


def table_rows(table):
    return -(-table.shape[1] * table.shape[2] // 8) * 8


def pack_kernel(one, two, table, out, sem):
    parts, branches, count, lanes = table.shape
    rows = (out.shape[1] - table_rows(table)) // 2
    copies = []
    for i, piece in enumerate((one, two)):
        source = piece.at[:, pl.ds(0, rows)]
        copies.append(begin(source, out.at[:, pl.ds(i * rows, rows)], sem.at[i]))
    for n in range(branches):
        row = 2 * rows + n * count
        for p in range(parts):
            out[0, row : row + count, p * lanes : (p + 1) * lanes] = table[p, n]
    for copy in copies:
        copy.wait()


def pack(one, two, table, rows):
    uppers, _, channels = one.shape
    out = jax.ShapeDtypeStruct((uppers, 2 * rows + table_rows(table), channels), F32)
    work = pl.CostEstimate(flops=0, bytes_accessed=16 * one.size, transcendentals=0)
    return call(pack_kernel, (out,), (one, two, table), [], 2, work)[0]


def next_kernel(lower, position, near, near_core, far, far_core, highs, lows, table, _):
    branches, channels, _ = highs.shape
    _, uppers, _, count, _ = near.shape
    for core, (near_blocks, far_blocks) in enumerate(((near, far), (near_core, far_core))):
        for j in range(3):
            block = lambda u, i: near_blocks[j, u, i]
            join(2 * j + core, lower, position[0], uppers, count, range(branches), block, highs, lows)
        block = lambda u, i: far_blocks[u, i * count : (i + 1) * count, :]
        join(6 + core, lower, position[0], uppers, count, range(branches), block, highs, lows)
    parts, _, taps, lanes = table.shape
    for n in range(branches):
        row = branches * count + n * taps
        for p in range(parts):
            table[p, n] = far[0, row : row + taps, p * lanes : (p + 1) * lanes]


def next_part(position, near, near_core, far, far_core, like, lower):
    table, highs, lows = (jax.ShapeDtypeStruct(w.shape, w.dtype) for w in like)
    work = pl.CostEstimate(flops=0, bytes_accessed=16 * near.size, transcendentals=0)
    operands = (position, near, near_core, far, far_core)
    kernel = functools.partial(next_kernel, lower)
    highs, lows, table = call(kernel, (highs, lows, table), operands, [], 1, work)
    return table, highs, lows


def ahead_kernel(position, newest, pair, highs, lows, *refs):
    taps, (out, table, earlier, sem) = refs[:2], refs[2:]
    load = begin(pair.at[0], earlier, sem.at[0])
    chip = position[0] // 2
    for j, part in enumerate(taps):
        for n in range(part.shape[0]):
            table[chip ^ j, n] = part[n]
    blocks = [chip // 2]
    total = separable(newest, table, highs, lows, 0, blocks)
    load.wait()
    out[...] = total + separable(earlier, table, highs, lows, 1, blocks)


def ahead_part(position, newest, pair, matrices, taps):
    shape, channels = newest.shape, newest.shape[-1]
    table = (channels // LANES,) + taps[0].shape
    return call(
        ahead_kernel,
        (jax.ShapeDtypeStruct(shape, F32),),
        (position, newest, pair, *matrices, *taps),
        [(table, F32), (shape, F32)],
        1,
        cost(shape, 1),
        apart=(2,),
    )[0]


def first_kernel(n_far, n_taps, n_sums, lower, position, newest, pair, highs_in, lows_in, *refs):
    far, taps, refs = refs[:n_far], refs[n_far : n_far + n_taps], refs[n_far + n_taps :]
    sums, (out, highs, lows, table, earlier, first, second, sem) = refs[:n_sums], refs[n_sums:]
    load = begin(pair.at[0], earlier, sem.at[0])
    branches, channels, _ = highs.shape
    chip = position[0] // 2
    if n_taps == 1:
        table[...] = taps[0][...]
    else:
        below = far[2]
        for j, part in enumerate(taps):
            row = below.shape[1] - (n_taps - j) * TAP_ROWS
            for n in range(branches):
                table[chip ^ j, n] = part[n]
                lanes = slice(n * LANES, (n + 1) * LANES)
                table[chip ^ (j + 2), n] = below[0, row : row + 9, lanes]
    join_far(far, lower, position[0], highs, lows)
    blocks = [1 - chip // 2] if sums else None
    total = separable(newest, table, highs, lows, 0, blocks)
    for part in sums:
        total = total + part[...]
    first[...] = total
    load.wait()
    first[...] += separable(earlier, table, highs, lows, 1, blocks)
    second[...] = separable(first, table, highs, lows, 2) + newest[...]
    out[...] = separable(second, table, highs, lows, 3) + first[...]


def first_part(position, newest, pair, matrices, far, lower, taps, sums):
    shape, channels = newest.shape, newest.shape[-1]
    branches = matrices[0].shape[0]
    lanes = min(LANES, channels)
    like = [jax.ShapeDtypeStruct(m.shape, m.dtype) for m in matrices]
    return call(
        functools.partial(first_kernel, len(far), len(taps), len(sums), lower),
        (
            jax.ShapeDtypeStruct(shape, F32),
            *like,
            jax.ShapeDtypeStruct((channels // lanes, branches, 9, lanes), F32),
        ),
        (position, newest, pair, *matrices, *far, *taps, *sums),
        [(shape, F32)] * 3,
        1,
        cost(shape, 4),
        apart=(2,),
        aliases={3: 1, 4: 2},
    )


def doubled(x, axis, bit, dim):
    other = swap(x, axis, bit)
    upper = (lax.axis_index(axis) & bit) != 0
    return jnp.where(upper, jnp.concatenate([other, x], dim), jnp.concatenate([x, other], dim))


def near_taps(taps, axis):
    size = lax.axis_size(axis)
    branches, count, width = taps.shape
    if size == 8 and 2 * width == LANES:
        return doubled(taps, axis, 1, 2)
    if size & (size - 1):
        taps = lax.all_gather(taps, axis, axis=2, tiled=True)
    else:
        bit = 1
        while bit < size:
            taps = doubled(taps, axis, bit, 2)
            bit *= 2
    channels = taps.shape[-1]
    lanes = min(LANES, channels)
    taps = taps.reshape(branches, count, channels // lanes, lanes)
    return taps.transpose(2, 0, 1, 3)


def from_neighbours(shard, axis):
    shard = shard[None]
    bit = 8
    while bit < lax.axis_size(axis):
        shard = doubled(shard, axis, bit, 0)
        bit *= 2
    return shard, swap(shard, axis, 2), swap(shard, axis, 4)


def body(pair, stems, taps, matrices):
    section = lax.axis_index("section").astype(jnp.int32).reshape(1)
    position = lax.axis_index("dp").astype(jnp.int32).reshape(1)
    stems = stems[:, 0]
    ticks = stems.shape[0] + 1
    pair = pair[0, :, 0]
    shard = matrices[0]
    newest = pair[1]
    size = lax.axis_size("dp")
    simple = size & (size - 1) or size < 8
    lower = 1 if simple else 8
    taps = near_taps(after(taps[0], section, position), "dp")
    newest, taps = lax.optimization_barrier((newest, taps))
    taps = (taps, swap(taps, "dp", 2)) if taps.ndim == 3 else (taps,)
    passed_on = from_behind(newest, "section", around=True)
    far = sums = ()
    channels = newest.shape[-1]
    if simple:
        partial = near_part(position, {0: lax.all_gather(shard, "dp")}, lower)
    else:
        own, x, y = from_neighbours(shard, "dp")
        near = {0: own, 1: swap(own, "dp", 1), 2: x, 4: y}
        two = half_of(after(x, near[1]), 1, *(taps if len(taps) > 1 else ()))
        one = half_of(y, 0)
        x_late, y_late = after(x, two), after(y, one)
        near.update({3: swap(x_late, "dp", 1), 5: swap(y_late, "dp", 1)})
        one, two = swap(one, "dp", 2), swap(two, "dp", 4)
        partial = near_part(position, near, lower)
        if len(taps) > 1 and channels == 2 * DEPTH:
            sums = (ahead_part(after(position, passed_on), newest, pair, partial, taps),)
        one, two, *_ = lax.optimization_barrier((one, two, passed_on, *partial, *sums))
        far = (one, swap(one, "dp", 1), two, swap(two, "dp", 1))
    output, *weights, table = first_part(
        position, newest, pair, partial, far, lower, taps, sums
    )
    weights = (table, *weights)

    if simple:
        next_shard = lax.all_gather(from_ahead(shard, "section"), "dp")
        next_weights = (from_ahead(table, "section"), *near_part(position, {0: next_shard}, lower))
    else:
        near = lax.optimization_barrier((own, x, y, *partial))[:3]
        next_near = from_ahead(stack(*near), "section")
        rows = far[0].shape[1]
    emitted = None
    held = (1, 0, newest)
    for tick in range(1, ticks - 1):
        earlier, newest, past = passed_on, from_behind(output, "section"), output
        if tick > 1:
            earlier = after(earlier, output)
        passed_on = from_behind(newest, "section", 1)
        early = early_part(tick, min(tick, 2), section, stems, earlier, weights)
        if tick == 1 and not simple:
            next_far = from_ahead(pack(after(far[0], early), far[2], table, rows), "section")
        emitted, output = late_part(
            tick, 1, section, stems, newest, early, weights, past, emitted, 12 if tick > 1 else 2
        )
        held = (tick, 1, newest)
        last_early = early

    if not simple:
        next_near, next_far, _ = lax.optimization_barrier((next_near, next_far, last_early))
        blocks = next_near, swap(next_near, "dp", 1), next_far, swap(next_far, "dp", 1)
        next_weights = next_part(position, *blocks, weights, lower)
    emitted, ahead = last_cell(
        held[0], held[1], section, stems, held[2], output, next_weights, emitted
    )
    got = from_behind(ahead, "section")
    emitted = last_part(section, got, stem_part(stems, weights), emitted)
    return emitted[None, :, None]


def solution(mesh):
    placed = (
        P("section", None, "dp", None, None, None),
        P(None, "dp", None, None, None),
        P("section", None, None, "dp"),
        P("section", None, "dp", None),
    )
    return jax.shard_map(
        body,
        mesh=mesh,
        in_specs=placed,
        out_specs=P("section", None, "dp", None, None, None),
        check_vma=False,
    )
```

```python
import functools

import jax
import jax.numpy as jnp
from jax import lax
from jax.experimental import pallas as pl
from jax.experimental.pallas import tpu as pltpu
from jax.sharding import PartitionSpec as P

F32 = jnp.float32
BF16 = jnp.bfloat16
VMEM_LIMIT = 16 * 1024 * 1024
LANES = 128
DEPTH = 256
TAP_ROWS = 16


def swap(x, axis, bit):
    size = lax.axis_size(axis)
    return lax.ppermute(x, axis, [(i, i ^ bit) for i in range(size)])


def from_behind(x, axis, first=0, around=False):
    size = lax.axis_size(axis)
    pairs = [(i, i + 1) for i in range(first, size - 1)]
    return lax.ppermute(x, axis, pairs + [(size - 1, 0)] * (around and size > 1))


def from_ahead(x, axis):
    return lax.ppermute(x, axis, [(i + 1, i) for i in range(lax.axis_size(axis) - 1)])


def after(x, *others):
    return lax.optimization_barrier((x, *others))[0]


def begin(source, target, sem):
    copy = pltpu.make_async_copy(source, target, sem)
    copy.start()
    return copy


def split(x):
    high = x.astype(BF16)
    return high, (x - high.astype(F32)).astype(BF16)


def call(kernel, outs, operands, scratch, copies, cost, apart=(), outs_apart=(), aliases=None, limit=VMEM_LIMIT):
    def spec(x, i, apart):
        space = pl.ANY if i in apart else pltpu.SMEM if x.dtype == jnp.int32 else pltpu.VMEM
        return pl.BlockSpec(memory_space=space)

    return pl.pallas_call(
        kernel,
        out_shape=outs,
        in_specs=[spec(x, i, apart) for i, x in enumerate(operands)],
        out_specs=tuple(spec(x, i, outs_apart) for i, x in enumerate(outs)),
        scratch_shapes=[pltpu.VMEM(*s) for s in scratch] + [pltpu.SemaphoreType.DMA((copies,))],
        input_output_aliases=aliases or {},
        compiler_params=pltpu.CompilerParams(vmem_limit_bytes=limit),
        cost_estimate=cost,
    )(*operands)


def cost(shape, convolutions):
    rows, columns, channels = shape
    size = rows * columns * channels
    return pl.CostEstimate(
        flops=6 * convolutions * size * channels,
        bytes_accessed=4 * (3 * size + convolutions * channels * channels),
        transcendentals=0,
    )


def shifted(u, by):
    side = u.shape[1]
    column = lax.broadcasted_iota(jnp.int32, u.shape, 1)
    outside = 0 if by == 1 else side - 1
    return jnp.where(column == outside, 0.0, pltpu.roll(u, by % side, 1))


def depthwise(source, table, branch, part, width):
    low = part * width
    if not isinstance(part, int):
        low = pl.multiple_of(low, width)
    x = jnp.maximum(source[:, :, pl.ds(low, width)], 0.0)
    nothing = jnp.zeros((1,) + x.shape[1:], F32)
    above = jnp.concatenate([nothing, x[:-1]], 0)
    below = jnp.concatenate([x[1:], nothing], 0)
    tap = [table[part, branch, k : k + 1, :].reshape(1, 1, width) for k in range(9)]
    by_column = [above * tap[j] + x * tap[3 + j] + below * tap[6 + j] for j in range(3)]
    return shifted(by_column[0], 1) + by_column[1] + shifted(by_column[2], -1)


def separable(source, table, highs, lows, branch, blocks=None):
    rows, columns, channels = source.shape
    width = min(LANES, channels)
    depth = min(DEPTH, channels)
    each = depth // width
    total = None
    for block in range(channels // depth) if blocks is None else blocks:
        mixed_in = []
        for i in range(each):
            value = depthwise(source, table, branch, block * each + i, width)
            mixed_in.append(split(value.reshape(rows * columns, width)))
        high = jnp.concatenate([p[0] for p in mixed_in], 1)
        low = jnp.concatenate([p[1] for p in mixed_in], 1)
        k = block * depth
        if not isinstance(block, int):
            k = pl.multiple_of(k, depth)
        matrix_high = highs[branch, pl.ds(k, depth), :]
        matrix_low = lows[branch, pl.ds(k, depth), :]
        both = jnp.concatenate([high, low], 0)
        product = jnp.dot(both, matrix_high, preferred_element_type=F32)
        product = product[: high.shape[0]] + product[high.shape[0] :]
        product = product + jnp.dot(high, matrix_low, preferred_element_type=F32)
        total = product if total is None else total + product
    return total.reshape(source.shape)


def fetch(tick, at, section, stems, got, held, sem):
    for s in range(at):

        @pl.when(section == s)
        def _(s=s):
            begin(stems.at[tick - 1 - s], held, sem)

    @pl.when(section >= at)
    def _():
        begin(got, held, sem)

    return pltpu.make_async_copy(got, held, sem)


def early_kernel(tick, at, section, stems, got, table, highs, lows, out, held, sem):
    fetch(tick, at, section[0], stems, got, held, sem.at[0]).wait()
    out[...] = separable(held, table, highs, lows, 1)


def late_kernel(tick, at, section, stems, got, early, table, highs, lows, past, *rest):
    emitted, out, newest, first, second, sem = rest[-6:]
    store = begin(past, emitted.at[tick - 1], sem.at[1])
    fetch(tick, at, section[0], stems, got, newest, sem.at[0]).wait()
    first[...] = separable(newest, table, highs, lows, 0) + early[...]
    second[...] = separable(first, table, highs, lows, 2) + newest[...]
    out[...] = separable(second, table, highs, lows, 3) + first[...]
    store.wait()


def early_part(tick, at, section, stems, got, weights):
    shape = got.shape
    return call(
        functools.partial(early_kernel, tick, at),
        (jax.ShapeDtypeStruct(shape, F32),),
        (section, stems, got, *weights),
        [(shape, F32)],
        1,
        cost(shape, 1),
        apart=(1, 2),
    )[0]


def late_part(tick, at, section, stems, got, early, weights, past, emitted, weight=2):
    shape = got.shape
    whole = jax.ShapeDtypeStruct((stems.shape[0] + 1,) + shape, F32)
    operands = (section, stems, got, early, *weights, past)
    return call(
        functools.partial(late_kernel, tick, at),
        (whole, jax.ShapeDtypeStruct(shape, F32)),
        operands if emitted is None else operands + (emitted,),
        [(shape, F32)] * 3,
        2,
        cost(shape, 3 * weight),
        apart=(1, 2, 8),
        outs_apart=(0,),
        aliases=None if emitted is None else {8: 0},
    )


def last_cell_kernel(tick, at, section, stems, got, newest, table, highs, lows, _, *rest):
    emitted, out, earlier, first, second, sem = rest
    load = fetch(tick, at, section[0], stems, got, earlier, sem.at[0])
    store = begin(newest, emitted.at[tick], sem.at[1])
    first[...] = separable(newest, table, highs, lows, 0)
    load.wait()
    first[...] += separable(earlier, table, highs, lows, 1)
    second[...] = separable(first, table, highs, lows, 2) + newest[...]
    out[...] = separable(second, table, highs, lows, 3) + first[...]
    store.wait()


def last_cell(tick, at, section, stems, got, newest, weights, emitted):
    shape = got.shape
    whole = jax.ShapeDtypeStruct(emitted.shape, F32)
    return call(
        functools.partial(last_cell_kernel, tick, at),
        (whole, jax.ShapeDtypeStruct(shape, F32)),
        (section, stems, got, newest, *weights, emitted),
        [(shape, F32)] * 3,
        2,
        cost(shape, 7),
        apart=(1, 2, 7),
        outs_apart=(0,),
        aliases={7: 0},
    )


def stem_kernel(stems, table, highs, lows, out, held, first, second, sem):
    begin(stems.at[stems.shape[0] - 1], held, sem.at[0]).wait()
    first[...] = separable(held, table, highs, lows, 0)
    first[...] += separable(held, table, highs, lows, 1)
    second[...] = separable(first, table, highs, lows, 2) + held[...]
    out[...] = separable(second, table, highs, lows, 3) + first[...]


def stem_part(stems, weights):
    shape = stems.shape[1:]
    a_map = jax.ShapeDtypeStruct(shape, F32)
    scratch = [(shape, F32)] * 3
    operands = (stems, *weights)
    return call(stem_kernel, (a_map,), operands, scratch, 1, cost(shape, 4), apart=(0,))[0]


def last_kernel(section, got, own, _, emitted, sem):
    target = emitted.at[emitted.shape[0] - 1]

    @pl.when(section[0] == 0)
    def _():
        begin(own, target, sem.at[0])

    @pl.when(section[0] > 0)
    def _():
        begin(got, target, sem.at[0])

    pltpu.make_async_copy(got, target, sem.at[0]).wait()


def last_part(section, got, own, emitted):
    whole = jax.ShapeDtypeStruct(emitted.shape, F32)
    work = pl.CostEstimate(flops=0, bytes_accessed=8 * got.size, transcendentals=0)
    operands = (section, got, own, emitted)
    return call(
        last_kernel, (whole,), operands, [], 1, work, apart=(3,), outs_apart=(0,), aliases={3: 0}
    )[0]


def join(key, lower, position, uppers, count, branches, block, highs, lows):
    for u in range(uppers):
        at = u * lower + ((position & (lower - 1)) ^ key)
        row = pl.multiple_of(at * count, count)
        for i in branches:
            high, low = split(block(u, i))
            highs[i, pl.ds(row, count), :] = high
            lows[i, pl.ds(row, count), :] = low


def near_kernel(keys, lower, position, *refs):
    pieces, (highs, lows, _) = refs[:-3], refs[-3:]
    for key, piece in zip(keys, pieces):
        uppers, branches, count, _ = piece.shape
        block = lambda u, i, piece=piece: piece[u, i]
        join(key, lower, position[0], uppers, count, range(branches), block, highs, lows)


def near_part(position, blocks, lower):
    uppers, branches, _, channels = blocks[0].shape
    matrices = jax.ShapeDtypeStruct((branches, channels, channels), BF16)
    return call(
        functools.partial(near_kernel, list(blocks), lower),
        (matrices, matrices),
        (position, *blocks.values()),
        [],
        1,
        pl.CostEstimate(flops=0, bytes_accessed=8 * matrices.size, transcendentals=0),
    )


def half_kernel(start, block, *refs):
    taps, (out, sem) = refs[:-2], refs[-2:]
    uppers, branches, count, _ = block.shape
    half = branches // 2
    copies = []
    for u in range(uppers):
        for i in range(half):
            target = out.at[u, pl.ds(i * count, count)]
            copies.append(begin(block.at[u, start + i], target, sem.at[u * half + i]))
    for j, chip in enumerate(taps):
        row = half * count + j * TAP_ROWS
        for n in range(branches):
            out[0, row : row + 9, n * LANES : (n + 1) * LANES] = chip[n]
    for copy in copies:
        copy.wait()


def half_of(block, start, *taps):
    uppers, branches, count, channels = block.shape
    half = branches // 2
    out = jax.ShapeDtypeStruct((uppers, half * count + TAP_ROWS * len(taps), channels), F32)
    work = pl.CostEstimate(flops=0, bytes_accessed=4 * block.size, transcendentals=0)
    kernel = functools.partial(half_kernel, start * half)
    return call(kernel, (out,), (block, *taps), [], half * uppers, work)[0]


def join_far(far, lower, position, highs, lows):
    branches, channels, _ = highs.shape
    half = branches // 2
    for j, piece in enumerate(far):
        uppers = piece.shape[0]
        count = channels // (uppers * lower)
        which = range(half) if j < 2 else range(half, branches)

        def block(u, i, piece=piece, which=which, count=count):
            at = (i - which[0]) * count
            return piece[u, at : at + count, :]

        join(6 + j % 2, lower, position, uppers, count, which, block, highs, lows)


def stack_kernel(*refs):
    pieces, (out, sem) = refs[:-2], refs[-2:]
    copies = [begin(piece, out.at[i], sem.at[i]) for i, piece in enumerate(pieces)]
    for copy in copies:
        copy.wait()


def stack(*pieces):
    n = len(pieces)
    out = jax.ShapeDtypeStruct((n,) + pieces[0].shape, F32)
    work = pl.CostEstimate(flops=0, bytes_accessed=8 * n * pieces[0].size, transcendentals=0)
    return call(stack_kernel, (out,), pieces, [], n, work, apart=range(n))[0]


def table_rows(table):
    return -(-table.shape[1] * table.shape[2] // 8) * 8


def pack_kernel(one, two, table, out, sem):
    parts, branches, count, lanes = table.shape
    rows = (out.shape[1] - table_rows(table)) // 2
    copies = []
    for i, piece in enumerate((one, two)):
        source = piece.at[:, pl.ds(0, rows)]
        copies.append(begin(source, out.at[:, pl.ds(i * rows, rows)], sem.at[i]))
    for n in range(branches):
        row = 2 * rows + n * count
        for p in range(parts):
            out[0, row : row + count, p * lanes : (p + 1) * lanes] = table[p, n]
    for copy in copies:
        copy.wait()


def pack(one, two, table, rows):
    uppers, _, channels = one.shape
    out = jax.ShapeDtypeStruct((uppers, 2 * rows + table_rows(table), channels), F32)
    work = pl.CostEstimate(flops=0, bytes_accessed=16 * one.size, transcendentals=0)
    return call(pack_kernel, (out,), (one, two, table), [], 2, work)[0]


def next_kernel(lower, position, near, near_core, far, far_core, highs, lows, table, _):
    branches, channels, _ = highs.shape
    _, uppers, _, count, _ = near.shape
    for core, (near_blocks, far_blocks) in enumerate(((near, far), (near_core, far_core))):
        for j in range(3):
            block = lambda u, i: near_blocks[j, u, i]
            join(2 * j + core, lower, position[0], uppers, count, range(branches), block, highs, lows)
        block = lambda u, i: far_blocks[u, i * count : (i + 1) * count, :]
        join(6 + core, lower, position[0], uppers, count, range(branches), block, highs, lows)
    parts, _, taps, lanes = table.shape
    for n in range(branches):
        row = branches * count + n * taps
        for p in range(parts):
            table[p, n] = far[0, row : row + taps, p * lanes : (p + 1) * lanes]


def next_part(position, near, near_core, far, far_core, like, lower):
    table, highs, lows = (jax.ShapeDtypeStruct(w.shape, w.dtype) for w in like)
    work = pl.CostEstimate(flops=0, bytes_accessed=16 * near.size, transcendentals=0)
    operands = (position, near, near_core, far, far_core)
    kernel = functools.partial(next_kernel, lower)
    highs, lows, table = call(kernel, (highs, lows, table), operands, [], 1, work)
    return table, highs, lows


def ahead_kernel(position, newest, pair, highs, lows, *refs):
    taps, (out, table, earlier, sem) = refs[:2], refs[2:]
    load = begin(pair.at[0], earlier, sem.at[0])
    chip = position[0] // 2
    for j, part in enumerate(taps):
        for n in range(part.shape[0]):
            table[chip ^ j, n] = part[n]
    blocks = [chip // 2]
    total = separable(newest, table, highs, lows, 0, blocks)
    load.wait()
    out[...] = total + separable(earlier, table, highs, lows, 1, blocks)


def ahead_part(position, newest, pair, matrices, taps):
    shape, channels = newest.shape, newest.shape[-1]
    table = (channels // LANES,) + taps[0].shape
    return call(
        ahead_kernel,
        (jax.ShapeDtypeStruct(shape, F32),),
        (position, newest, pair, *matrices, *taps),
        [(table, F32), (shape, F32)],
        1,
        cost(shape, 1),
        apart=(2,),
    )[0]


def first_kernel(n_far, n_taps, n_sums, lower, position, newest, pair, highs_in, lows_in, *refs):
    far, taps, refs = refs[:n_far], refs[n_far : n_far + n_taps], refs[n_far + n_taps :]
    sums, (out, highs, lows, table, earlier, first, second, sem) = refs[:n_sums], refs[n_sums:]
    load = begin(pair.at[0], earlier, sem.at[0])
    branches, channels, _ = highs.shape
    chip = position[0] // 2
    if n_taps == 1:
        table[...] = taps[0][...]
    else:
        below = far[2]
        for j, part in enumerate(taps):
            row = below.shape[1] - (n_taps - j) * TAP_ROWS
            for n in range(branches):
                table[chip ^ j, n] = part[n]
                lanes = slice(n * LANES, (n + 1) * LANES)
                table[chip ^ (j + 2), n] = below[0, row : row + 9, lanes]
    join_far(far, lower, position[0], highs, lows)
    blocks = [1 - chip // 2] if sums else None
    total = separable(newest, table, highs, lows, 0, blocks)
    for part in sums:
        total = total + part[...]
    first[...] = total
    load.wait()
    first[...] += separable(earlier, table, highs, lows, 1, blocks)
    second[...] = separable(first, table, highs, lows, 2) + newest[...]
    out[...] = separable(second, table, highs, lows, 3) + first[...]


def first_part(position, newest, pair, matrices, far, lower, taps, sums):
    shape, channels = newest.shape, newest.shape[-1]
    branches = matrices[0].shape[0]
    lanes = min(LANES, channels)
    like = [jax.ShapeDtypeStruct(m.shape, m.dtype) for m in matrices]
    return call(
        functools.partial(first_kernel, len(far), len(taps), len(sums), lower),
        (
            jax.ShapeDtypeStruct(shape, F32),
            *like,
            jax.ShapeDtypeStruct((channels // lanes, branches, 9, lanes), F32),
        ),
        (position, newest, pair, *matrices, *far, *taps, *sums),
        [(shape, F32)] * 3,
        1,
        cost(shape, 4),
        apart=(2,),
        aliases={3: 1, 4: 2},
    )


def doubled(x, axis, bit, dim):
    other = swap(x, axis, bit)
    upper = (lax.axis_index(axis) & bit) != 0
    return jnp.where(upper, jnp.concatenate([other, x], dim), jnp.concatenate([x, other], dim))


def near_taps(taps, axis):
    size = lax.axis_size(axis)
    branches, count, width = taps.shape
    if size == 8 and 2 * width == LANES:
        return doubled(taps, axis, 1, 2)
    if size & (size - 1):
        taps = lax.all_gather(taps, axis, axis=2, tiled=True)
    else:
        bit = 1
        while bit < size:
            taps = doubled(taps, axis, bit, 2)
            bit *= 2
    channels = taps.shape[-1]
    lanes = min(LANES, channels)
    taps = taps.reshape(branches, count, channels // lanes, lanes)
    return taps.transpose(2, 0, 1, 3)


def from_neighbours(shard, axis):
    shard = shard[None]
    bit = 8
    while bit < lax.axis_size(axis):
        shard = doubled(shard, axis, bit, 0)
        bit *= 2
    return shard, swap(shard, axis, 2), swap(shard, axis, 4)


def body(pair, stems, taps, matrices):
    section = lax.axis_index("section").astype(jnp.int32).reshape(1)
    position = lax.axis_index("dp").astype(jnp.int32).reshape(1)
    stems = stems[:, 0]
    ticks = stems.shape[0] + 1
    pair = pair[0, :, 0]
    shard = matrices[0]
    newest = pair[1]
    size = lax.axis_size("dp")
    simple = size & (size - 1) or size < 8
    lower = 1 if simple else 8
    taps = near_taps(after(taps[0], section, position), "dp")
    newest, taps = lax.optimization_barrier((newest, taps))
    taps = (taps, swap(taps, "dp", 2)) if taps.ndim == 3 else (taps,)
    passed_on = from_behind(newest, "section", around=True)
    far = sums = ()
    channels = newest.shape[-1]
    if simple:
        partial = near_part(position, {0: lax.all_gather(shard, "dp")}, lower)
    else:
        own, x, y = from_neighbours(shard, "dp")
        near = {0: own, 1: swap(own, "dp", 1), 2: x, 4: y}
        two = half_of(x, 1, *(taps if len(taps) > 1 else ()))
        one = half_of(y, 0)
        x_late, y_late = after(x, two), after(y, one)
        near.update({3: swap(x_late, "dp", 1), 5: swap(y_late, "dp", 1)})
        one, two = swap(one, "dp", 2), swap(two, "dp", 4)
        partial = near_part(position, near, lower)
        if len(taps) > 1 and channels == 2 * DEPTH:
            sums = (ahead_part(after(position, passed_on), newest, pair, partial, taps),)
        one, two, *_ = lax.optimization_barrier((one, two, passed_on, *partial, *sums))
        far = (one, swap(one, "dp", 1), two, swap(two, "dp", 1))
    output, *weights, table = first_part(
        position, newest, pair, partial, far, lower, taps, sums
    )
    weights = (table, *weights)

    if simple:
        next_shard = lax.all_gather(from_ahead(shard, "section"), "dp")
        next_weights = (from_ahead(table, "section"), *near_part(position, {0: next_shard}, lower))
    else:
        near = lax.optimization_barrier((own, x, y, *partial))[:3]
        next_near = from_ahead(stack(*near), "section")
        rows = far[0].shape[1]
    emitted = None
    held = (1, 0, newest)
    for tick in range(1, ticks - 1):
        earlier, newest, past = passed_on, from_behind(output, "section"), output
        if tick > 1:
            earlier = after(earlier, output)
        passed_on = from_behind(newest, "section", 1)
        early = early_part(tick, min(tick, 2), section, stems, earlier, weights)
        if tick == 1 and not simple:
            next_far = from_ahead(pack(after(far[0], early), far[2], table, rows), "section")
        emitted, output = late_part(
            tick, 1, section, stems, newest, early, weights, past, emitted, 12 if tick > 1 else 2
        )
        held = (tick, 1, newest)
        last_early = early

    if not simple:
        next_near, next_far, _ = lax.optimization_barrier((next_near, next_far, last_early))
        blocks = next_near, swap(next_near, "dp", 1), next_far, swap(next_far, "dp", 1)
        next_weights = next_part(position, *blocks, weights, lower)
    emitted, ahead = last_cell(
        held[0], held[1], section, stems, held[2], output, next_weights, emitted
    )
    got = from_behind(ahead, "section")
    emitted = last_part(section, got, stem_part(stems, weights), emitted)
    return emitted[None, :, None]


def solution(mesh):
    placed = (
        P("section", None, "dp", None, None, None),
        P(None, "dp", None, None, None),
        P("section", None, None, "dp"),
        P("section", None, "dp", None),
    )
    return jax.shard_map(
        body,
        mesh=mesh,
        in_specs=placed,
        out_specs=P("section", None, "dp", None, None, None),
        check_vma=False,
    )
```
